768 devices in a mesh: sec: 4 (over y_lo), sp: 8 (over x, core), dp: 24 (over y_hi, z).
Axes of the slice: x: 4, y: 8 (y_hi: 2, y_lo: 4; y = y_hi * 4 + y_lo), z: 12, core: 2. Of those that a mesh axis runs over, the one named last changes fastest.
Arguments:
- fraction: float32 [24, 32, 32, 1024], P('dp', None, 'sp', 'sec'), may hold values from 0 to 1
- labels: int32 [24, 32, 32, 1024], P('dp', ('sec', 'sp')), may hold values from 0 to 63
- conv_weight: bfloat16 [54, 64], replicated, may hold values from -6 to 6
- conv_bias: float32 [64], replicated, may hold values from -6 to 6
- out_weight: bfloat16 [64, 64], replicated, may hold values from -6 to 6
- out_bias: float32 [64], replicated, may hold values from -6 to 6
Outputs:
- cell_loss: float32 [24, 32, 32, 1024], P('dp', ('sec', 'sp'))
- conv_weight_grad: float32 [54, 64], replicated
- conv_bias_grad: float32 [64], replicated
- out_weight_grad: float32 [64, 64], replicated
- out_bias_grad: float32 [64], replicated
The draws below stay inside these ranges and needn't reach their ends.
All inputs are finite; a program needn't handle non-finite values.
Results may differ from the reference program's by a relative error of at most 0.00035.
The reference program's roundings to bfloat16 on the way (of `features`, `columns`, `hidden_act`, `residual_low` and `hidden_low`) count: a program that leaves them out, or rounds other values in their place, can miss the bound.
Values may be sent and summed in bfloat16 or wider, within the bound.
A program may use at most 32 MiB of HBM per device.

```python
import jax
import jax.numpy as jnp
from jax import lax

PX = 32
PY = 32
PZ = 32
HID = 64
BINS = 64
GROUPS = 24
GP = 32
PLANE = 1024
FEATS = 54
CELLS_ALL = 25165824


def plant(array, key, least, top_value):
    longest = array.shape.index(max(array.shape))
    spots = []
    for shift in (0, 1):
        where = [jax.random.randint(jax.random.fold_in(key, axis), (), 0, length) for axis, length in enumerate(array.shape)]
        where[longest] = (where[longest] + shift) % array.shape[longest]
        spots.append(tuple(where))
    return array.at[spots[0]].set(least).at[spots[1]].set(top_value)


def levels(stream_key, extent, pieces, low, largest):
    level, own = 1.0, jax.random.fold_in(stream_key, 6)
    for dim, parts in pieces:
        heights = jnp.exp(jax.random.uniform(jax.random.fold_in(own, dim), (parts,), jnp.float32, low / len(pieces), largest / len(pieces)))
        level = level * jnp.repeat(heights, extent[dim] // parts).reshape([-1 if axis == dim else 1 for axis in range(len(extent))])
    return level


def normal_values(rng, dims, scale, reach, held_as=jnp.bfloat16):
    return jnp.clip(scale * jax.random.normal(rng, dims, jnp.float32), -reach, reach).astype(held_as)


def setup_inputs(seed: int = 0) -> dict:
    splits = jax.random.split(jax.random.key(seed), 7)
    return {
        "fraction": jnp.clip(1.0 * jax.random.uniform(splits[0], (GROUPS, GP, PX, PLANE), jnp.float32) ** levels(splits[0], (GROUPS, GP, PX, PLANE), ((0, 24), (2, 8), (3, 4)), -0.2, 0.2), 0.0, 1.0),
        "labels": plant(jax.random.randint(splits[1], (GROUPS, GP, PX, PLANE), 0, BINS), jax.random.fold_in(splits[1], 1), 0, BINS - 1).astype(jnp.int32),
        "conv_weight": normal_values(splits[2], (FEATS, HID), 0.5, 6.0),
        "conv_bias": normal_values(splits[3], (HID,), 1.0, 6.0, jnp.float32),
        "out_weight": normal_values(splits[4], (HID, BINS), 0.4, 6.0),
        "out_bias": normal_values(splits[5], (BINS,), 1.0, 6.0, jnp.float32),
    }


def shift_cells(values, offset, step_y, step_z):
    length = values.shape[-1]
    margin = PY * PZ + PZ + 1
    widths = [(0, 0)] * (values.ndim - 1) + [(margin, margin)]
    padded = jnp.pad(values, widths)
    shifted = lax.slice_in_dim(padded, margin + offset, margin + offset + length, axis=values.ndim - 1)
    position = jnp.arange(length, dtype=jnp.int32)
    row_y = (position // PZ) % PY + step_y
    col_z = position % PZ + step_z
    inside = (row_y >= 0) & (row_y < PY) & (col_z >= 0) & (col_z < PZ)
    return jnp.where(inside, shifted, jnp.zeros((), values.dtype))


def box_filter(padded):
    x_sums = padded[..., :-2, :] + padded[..., 1:-1, :] + padded[..., 2:, :]
    window_sum = jnp.zeros_like(x_sums)
    for step_y in (-1, 0, 1):
        for step_z in (-1, 0, 1):
            window_sum = window_sum + shift_cells(x_sums, step_y * PZ + step_z, step_y, step_z)
    return window_sum / 27.0


def make_columns(features):
    shifted_list = []
    for step_x in (-1, 0, 1):
        for step_y in (-1, 0, 1):
            for step_z in (-1, 0, 1):
                offset = step_x * PY * PZ + step_y * PZ + step_z
                shifted_list.append(shift_cells(features, offset, step_y, step_z))
    stacked = jnp.stack(shifted_list)
    return stacked.reshape(2 * stacked.shape[0], stacked.shape[2])


def patch_step(features, patch_labels, conv_weight, conv_bias, out_weight, out_bias, weight_scale):
    columns = make_columns(features)
    columns_wide = columns.astype(jnp.float32)
    hidden_pre = jnp.einsum("kc,kh->hc", columns_wide, conv_weight.astype(jnp.float32)) + conv_bias[:, None]
    hidden_act = lax.optimization_barrier(jax.nn.silu(hidden_pre).astype(jnp.bfloat16))
    act_wide = hidden_act.astype(jnp.float32)
    logits = jnp.einsum("hb,hc->bc", out_weight.astype(jnp.float32), act_wide) + out_bias[:, None]
    exp_logits = jnp.exp(logits)
    partition = jnp.sum(exp_logits, axis=0)
    bin_ids = jnp.arange(logits.shape[0], dtype=jnp.int32)[:, None]
    is_label = bin_ids == patch_labels[None, :]
    cell_term = jnp.log(partition) - jnp.sum(jnp.where(is_label, logits, jnp.zeros((), logits.dtype)), axis=0)
    residual = (exp_logits / partition - is_label.astype(jnp.float32)) * weight_scale
    residual_low = lax.optimization_barrier(residual.astype(jnp.bfloat16)).astype(jnp.float32)
    out_weight_grad = jnp.einsum("hc,bc->hb", act_wide, residual_low)
    out_bias_grad = jnp.sum(residual, axis=1)
    hidden_back = jnp.einsum("hb,bc->hc", out_weight.astype(jnp.float32), residual_low)
    sigmoid_pre = jax.nn.sigmoid(hidden_pre)
    hidden_grad = hidden_back * sigmoid_pre * (1.0 + hidden_pre * (1.0 - sigmoid_pre))
    conv_bias_grad = jnp.sum(hidden_grad, axis=1)
    hidden_low = lax.optimization_barrier(hidden_grad.astype(jnp.bfloat16)).astype(jnp.float32)
    conv_weight_grad = jnp.einsum("kc,hc->kh", columns_wide, hidden_low)
    return cell_term, (conv_weight_grad, conv_bias_grad, out_weight_grad, out_bias_grad)


def reference(fraction, labels, conv_weight, conv_bias, out_weight, out_bias):
    patches = fraction.reshape(-1, PX, PY * PZ)
    moments = jnp.stack([patches, patches * patches])
    padded = jnp.pad(moments, ((0, 0), (0, 0), (1, 1), (0, 0)))
    filtered = box_filter(padded)
    mean_part = filtered[0]
    spread = filtered[1] - mean_part * mean_part
    features = lax.optimization_barrier(jnp.stack([mean_part, spread], axis=1).astype(jnp.bfloat16))
    features = features.reshape(features.shape[0], 2, PX * PY * PZ)
    flat_labels = labels.reshape(-1, PX * PY * PZ)
    weight_scale = 1.0 / CELLS_ALL
    initial = (jnp.zeros((FEATS, HID), jnp.float32), jnp.zeros((HID,), jnp.float32),
               jnp.zeros((HID, BINS), jnp.float32), jnp.zeros((BINS,), jnp.float32))

    def accumulate(running, patch_item):
        cell_term, terms = patch_step(patch_item[0], patch_item[1], conv_weight, conv_bias,
                                      out_weight, out_bias, weight_scale)
        return tuple(left + right for left, right in zip(running, terms)), cell_term

    totals, losses = lax.scan(accumulate, initial, (features, flat_labels))
    cell_loss = losses.reshape(labels.shape)
    return (cell_loss, totals[0], totals[1], totals[2], totals[3])
```

```python
import functools
import jax
import jax.numpy as jnp
from jax import lax
from jax.experimental import pallas as pl
from jax.experimental.pallas import tpu as pltpu
from jax.sharding import PartitionSpec as P

PX, PY, PZ = 32, 32, 32
PLANE = PY * PZ
HID = 64
BINS = 64
FEATS = 54
XB = 8
NB = PX // XB
GROUP = 24
KC = 9 * GROUP
KP = KC + 8
KO = HID + 16
TILE = 256
F32, BF16 = jnp.float32, jnp.bfloat16
LEAD = 3
CH = 2
NT = (((1,), (1,)), ((), ()))
TN = (((0,), (0,)), ((), ()))


def iota(shape, axis):
    return lax.broadcasted_iota(jnp.int32, shape, axis)


def split3(value):
    high = value.astype(BF16)
    rest = value - high.astype(F32)
    mid = rest.astype(BF16)
    low = (rest - mid.astype(F32)).astype(BF16)
    return high.astype(F32), mid.astype(F32), low.astype(F32)


def column(row):
    n = row.shape[1]
    eye = iota((n, n), 0) == iota((n, n), 1)
    return jnp.sum(jnp.where(eye, row, 0.0), axis=1, keepdims=True)


def conv_rows(p_minus_x, shape, k_axis, c_axis):
    col = iota(shape, c_axis)
    k = iota(shape, k_axis)
    t = col // GROUP
    u = col - t * GROUP
    c = jnp.where(u >= 10, 1, 0)
    dx = u - 10 * c - p_minus_x
    return (col < KC) & (u < 20) & (dx >= 0) & (dx < 3) & (k == 18 * dx + 2 * t + c)


def prepare(cw_ref, cb_ref, ow_ref, ob_ref, wide_ref, owt_ref, owb_ref):
    cb = column(cb_ref[...].reshape(1, HID)) * 0.5
    ch, cm, cl = split3(cb)
    col = iota((HID, KP), 1)
    bias = jnp.where(col == KC, ch, jnp.where(col == KC + 1, cm, jnp.where(col == KC + 2, cl, 0.0)))
    cw = cw_ref[...]
    for x in range(XB):
        pick = jnp.where(conv_rows(x, (FEATS, KP), 0, 1), 0.5, 0.0).astype(BF16)
        row = lax.dot_general(cw, pick, TN, preferred_element_type=F32) + bias
        wide_ref[x * HID:(x + 1) * HID, :] = row.astype(BF16)
    ob = column(ob_ref[...].reshape(1, BINS))
    oh, om, ol = split3(ob)
    ow = ow_ref[...]
    eye = (iota((HID, KO), 0) == iota((HID, KO), 1)).astype(F32).astype(BF16)
    owt = lax.dot_general(ow, eye, TN, preferred_element_type=F32)
    col = iota((BINS, KO), 1)
    owt = owt + jnp.where(col == HID, oh, jnp.where(col == HID + 1, om, jnp.where(col == HID + 2, ol, 0.0)))
    owt_ref[...] = owt.astype(BF16)
    owb_ref[...] = (ow.astype(F32) * 0.5).astype(BF16)


def box(padded_ref, square, z_lo, z_hi, y_lo, y_hi):
    a, b, c = padded_ref[7:39, :], padded_ref[8:40, :], padded_ref[9:41, :]
    if square:
        s = a * a + b * b + c * c
    else:
        s = a + b + c
    s = s + jnp.where(z_lo, 0.0, pltpu.roll(s, 1, 1)) + jnp.where(z_hi, 0.0, pltpu.roll(s, PLANE - 1, 1))
    s = s + jnp.where(y_lo, 0.0, pltpu.roll(s, PZ, 1)) + jnp.where(y_hi, 0.0, pltpu.roll(s, PLANE - PZ, 1))
    return s / 27.0


def edges(shape):
    pos = iota(shape, 1)
    z = pos & (PZ - 1)
    return z == 0, z == PZ - 1, pos < PZ, pos >= PLANE - PZ


def filter_patch(patch_ref, pad_ref, f0_ref, f1_ref):
    zero = jnp.zeros((8, PLANE), F32)
    for ref in (pad_ref, f0_ref, f1_ref):
        ref[0:8, :] = zero
        ref[40:48, :] = zero
    for i in range(8):
        pad_ref[8 + 4 * i:12 + 4 * i, :] = patch_ref[i]
    z_lo, z_hi, y_lo, y_hi = edges((PX, PLANE))
    filt = box(pad_ref, False, z_lo, z_hi, y_lo, y_hi)
    f0_ref[8:40, :] = filt
    f1_ref[8:40, :] = box(pad_ref, True, z_lo, z_hi, y_lo, y_hi) - filt * filt


def stencil(f0_ref, f1_ref, join_ref, g_ref):
    z_lo, z_hi, y_lo, y_hi = edges((GROUP, PLANE))
    join_ref[20:24, :] = jnp.zeros((4, PLANE), F32)
    for b in range(NB):
        join_ref[0:10, :] = f0_ref[8 * b + 7:8 * b + 17, :]
        join_ref[10:20, :] = f1_ref[8 * b + 7:8 * b + 17, :]
        mid = join_ref[...]
        lo = jnp.where(z_lo, 0.0, pltpu.roll(mid, 1, 1))
        hi = jnp.where(z_hi, 0.0, pltpu.roll(mid, PLANE - 1, 1))
        parts = []
        for step_y in (-1, 0, 1):
            for v in (lo, mid, hi):
                if step_y == -1:
                    v = jnp.where(y_lo, 0.0, pltpu.roll(v, PZ, 1))
                elif step_y == 1:
                    v = jnp.where(y_hi, 0.0, pltpu.roll(v, PLANE - PZ, 1))
                parts.append(v)
        parts.append(jnp.ones((8, PLANE), F32))
        g_ref[b] = jnp.concatenate(parts, axis=0).astype(BF16)


def fold(v):
    return v[:, :128] + v[:, 128:]


def train(labels_ref, wide_ref, owt_ref, owb_ref, g_ref, act_ref, d_ref, low_ref, grad_ref, z_ref, pick_ref, dconv_ref, dout_ref, hsum_ref, rsum_ref, scale):
    dconv_ref[...] = jnp.zeros_like(dconv_ref)
    dout_ref[...] = jnp.zeros_like(dout_ref)
    hsum_ref[...] = jnp.zeros_like(hsum_ref)
    rsum_ref[...] = jnp.zeros_like(rsum_ref)
    low_ref[...] = jnp.zeros_like(low_ref)
    grad_ref[...] = jnp.zeros_like(grad_ref)
    act_ref[...] = jnp.zeros_like(act_ref)
    bins = iota((BINS, TILE), 0)
    ones = jnp.ones((16, TILE), BF16)
    width = CH * TILE
    per = PLANE // width
    steps = NB * per

    def place(step, c):
        b = step // per
        return b, pl.ds(pl.multiple_of((step % per) * width + c * TILE, TILE), TILE)

    def whole(step):
        b = step // per
        return b, pl.ds(pl.multiple_of((step % per) * width, width), width)

    def ahead(step, slot, c):
        b, cols = place(step, c)
        u_all = jnp.dot(wide_ref[...], g_ref[b, :, cols], preferred_element_type=F32)
        for x in range(XB):
            u = u_all[x * HID:(x + 1) * HID]
            t = jnp.tanh(u)
            w = 1.0 + t
            a = u * w
            act_ref[slot, x, :, c * TILE:(c + 1) * TILE] = a.astype(BF16)
            d_ref[slot, x, :, c * TILE:(c + 1) * TILE] = (w + a) - a * t

    def behind_out(step, act_slot, slot):
        dout_ref[...] += lax.dot_general(
            jnp.concatenate([act_ref[act_slot, x] for x in range(XB)], axis=1),
            jnp.concatenate([low_ref[slot, x] for x in range(XB)], axis=1), NT, preferred_element_type=F32)

    def behind_conv(step, slot):
        b, cols = whole(step)
        dconv_ref[...] += lax.dot_general(grad_ref[slot], g_ref[b, :, cols], NT, preferred_element_type=F32)

    for c in range(CH):
        ahead(0, 0, c)

    def body(step, carry):
        slot = lax.rem(step, 2)
        slot3 = lax.rem(step, 3)
        next3 = lax.rem(step + 1, 3)
        last3 = lax.rem(step + 2, 3)
        last = jnp.maximum(step - 1, 0)

        def project(c, x):
            return jnp.dot(owt_ref[...], jnp.concatenate([act_ref[slot3, x, :, c * TILE:(c + 1) * TILE], ones], axis=0), preferred_element_type=F32)

        tiles = [(c, x) for c in range(CH) for x in range(XB)]
        count = len(tiles)
        logits_of = {i: project(*tiles[i]) for i in range(LEAD)}
        backs = {}
        hsum = rsum = None
        for i in range(count + 1):
            if i < count:
                c, x = tiles[i]
                span = slice(c * TILE, (c + 1) * TILE)
                b, cols = place(step, c)
                logits = logits_of.pop(i)
                if i + LEAD < count:
                    logits_of[i + LEAD] = project(*tiles[i + LEAD])
                if i % XB == 0:
                    ahead_at(ahead, step, next3, c, steps)
                e = jnp.exp(logits)
                row = XB * b + x
                hit = bins == labels_ref[pl.ds(row, 1), cols]
                total = jnp.sum(e, axis=0, keepdims=True)
                z_ref[pl.ds(row, 1), cols] = total
                pick_ref[pl.ds(row, 1), cols] = jnp.sum(jnp.where(hit, logits, 0.0), axis=0, keepdims=True)
                r = e * (scale / total) - jnp.where(hit, scale, 0.0)
                low = r.astype(BF16)
                low_ref[slot, x, :, span] = low
                rsum = fold(r) if rsum is None else rsum + fold(r)
                backs[i] = jnp.dot(owb_ref[...], low, preferred_element_type=F32)
                if i == count // 4:
                    behind_out(last, last3, 1 - slot)
                if i == count // 2:
                    behind_conv(last, 1 - slot)
            if i >= 1:
                c, x = tiles[i - 1]
                span = slice(c * TILE, (c + 1) * TILE)
                grad = backs.pop(i - 1) * d_ref[slot3, x, :, span]
                grad_ref[slot, x * HID:(x + 1) * HID, span] = grad.astype(BF16)
                hsum = fold(grad) if hsum is None else hsum + fold(grad)
        hsum_ref[...] += hsum
        rsum_ref[...] += rsum
        return carry

    lax.fori_loop(0, steps, body, 0)
    behind_out(steps - 1, (steps - 1) % 3, (steps - 1) % 2)
    behind_conv(steps - 1, (steps - 1) % 2)


def ahead_at(ahead, step, slot, c, steps):
    ahead(jnp.minimum(step + 1, steps - 1), slot, c)


def finish(z_ref, pick_ref, dconv_ref, dout_ref, hsum_ref, rsum_ref, loss_ref, part_ref):
    loss_ref[...] = jnp.log(z_ref[...]) - pick_ref[...]
    total = dconv_ref[0:HID, :]
    for x in range(1, XB):
        total = total + pltpu.roll(dconv_ref[x * HID:(x + 1) * HID, :], KP - x, 1)
    col = iota((HID, KP), 1)
    hcol = jnp.sum(hsum_ref[...], axis=1, keepdims=True)
    rcol = jnp.sum(rsum_ref[...], axis=1, keepdims=True)
    total = jnp.where(col == KC, hcol, jnp.where(col == KC + 1, rcol, total))
    k, c = iota((HID, KP), 0), iota((HID, KP), 1)
    pick = conv_rows(0, (HID, KP), 0, 1) | ((k == FEATS) & (c == KC)) | ((k == FEATS + 1) & (c == KC + 1))
    rows = lax.dot_general(jnp.where(pick, 1.0, 0.0), total, NT, precision=lax.Precision.HIGHEST, preferred_element_type=F32)
    part_ref[:, 0:HID] = rows
    part_ref[:, HID:2 * HID] = dout_ref[...]


def compute_scratch():
    return [
        pltpu.VMEM((48, PLANE), F32), pltpu.VMEM((48, PLANE), F32), pltpu.VMEM((48, PLANE), F32),
        pltpu.VMEM((GROUP, PLANE), F32),
        pltpu.VMEM((NB, KP, PLANE), BF16),
        pltpu.VMEM((XB * HID, KP), BF16), pltpu.VMEM((BINS, KO), BF16), pltpu.VMEM((HID, BINS), BF16),
        pltpu.VMEM((3, XB, HID, CH * TILE), BF16), pltpu.VMEM((3, XB, HID, CH * TILE), F32),
        pltpu.VMEM((2, XB, BINS, CH * TILE), BF16), pltpu.VMEM((2, XB * HID, CH * TILE), BF16),
        pltpu.VMEM((PX, PLANE), F32), pltpu.VMEM((PX, PLANE), F32),
        pltpu.VMEM((XB * HID, KP), F32), pltpu.VMEM((HID, BINS), F32),
        pltpu.VMEM((HID, 128), F32), pltpu.VMEM((BINS, 128), F32),
    ]


def compute_kernel(scale, stages, patch_ref, labels_ref, cw_ref, cb_ref, ow_ref, ob_ref, loss_ref, part_ref,
                   pad, f0, f1, join, g, wide, owt, owb, act, d, low, grad, z, pick, dconv, dout, hsum, rsum):
    if "p" in stages:
        prepare(cw_ref, cb_ref, ow_ref, ob_ref, wide, owt, owb)
    if "f" in stages:
        filter_patch(patch_ref, pad, f0, f1)
    if "s" in stages:
        stencil(f0, f1, join, g)
    if "t" in stages:
        train(labels_ref, wide, owt, owb, g, act, d, low, grad, z, pick, dconv, dout, hsum, rsum, scale)
    if "e" in stages:
        finish(z, pick, dconv, dout, hsum, rsum, loss_ref, part_ref)


def compute(patch, labels, cw, cb, ow, ob, scale, stages="pfste"):
    vm = pl.BlockSpec(memory_space=pltpu.VMEM)
    return pl.pallas_call(
        functools.partial(compute_kernel, scale, stages),
        out_shape=(jax.ShapeDtypeStruct((PX, PLANE), F32), jax.ShapeDtypeStruct((HID, 128), F32)),
        in_specs=[vm] * 6,
        out_specs=(vm, vm),
        scratch_shapes=compute_scratch(),
        compiler_params=pltpu.CompilerParams(vmem_limit_bytes=48 * 2**20),
        name="train_patch",
    )(patch, labels, cw, cb, ow, ob)


SEC, SP, DP = 4, 8, 24
TEAM = SEC * SP
PIECE = HID // TEAM


def team_rank():
    return lax.axis_index("sec") * SP + lax.axis_index("sp")


def team_device(rank):
    return {"sec": rank // SP, "sp": rank % SP}


def greet(team, replicas):
    barrier = pltpu.get_barrier_semaphore()
    if team:
        me = team_rank()

        def hail(i, carry):
            pl.semaphore_signal(barrier, inc=1, device_id=team_device(lax.rem(me + i, TEAM)), device_id_type=pl.DeviceIdType.MESH)
            return carry

        lax.fori_loop(1, TEAM, hail, 0)
    if replicas:
        mine = lax.axis_index("dp")

        def call(i, carry):
            pl.semaphore_signal(barrier, inc=1, device_id={"dp": lax.rem(mine + i, DP)}, device_id_type=pl.DeviceIdType.MESH)
            return carry

        lax.fori_loop(1, DP, call, 0)
    pl.semaphore_wait(barrier, (TEAM - 1) * team + (DP - 1) * replicas)


def relay_kernel(frac_ref, patch_ref, own_sem, send_sems, recv_sems):
    greet(1, 0)
    me = team_rank()
    sec, sp = lax.axis_index("sec"), lax.axis_index("sp")
    spot = patch_ref.at[sp, :, pl.ds(pl.multiple_of(sec * TILE, TILE), TILE)]

    def parcel(rank, sender):
        return pltpu.make_async_remote_copy(
            src_ref=frac_ref.at[rank], dst_ref=spot, send_sem=send_sems.at[rank], recv_sem=recv_sems.at[sender],
            device_id=team_device(rank), device_id_type=pl.DeviceIdType.MESH)

    def send(i, carry):
        parcel(lax.rem(me + i, TEAM), me).start()
        return carry

    lax.fori_loop(1, TEAM, send, 0)
    own = pltpu.make_async_copy(frac_ref.at[me], spot, own_sem)
    own.start()

    def settle(i, carry):
        other = lax.rem(me + i, TEAM)
        parcel(other, other).wait()
        return carry

    lax.fori_loop(1, TEAM, settle, 0)
    own.wait()


def relay(frac):
    return pl.pallas_call(
        relay_kernel,
        out_shape=jax.ShapeDtypeStruct((SP, 4, PLANE), F32),
        in_specs=[pl.BlockSpec(memory_space=pl.ANY)],
        out_specs=pl.BlockSpec(memory_space=pltpu.VMEM),
        scratch_shapes=[pltpu.SemaphoreType.DMA, pltpu.SemaphoreType.DMA((TEAM,)), pltpu.SemaphoreType.DMA((TEAM,))],
        compiler_params=pltpu.CompilerParams(collective_id=0, has_side_effects=True),
        name="relay_patches",
    )(frac)


def swap(ref, slots, sends, recvs, count, me, device, source):
    def parcel(rank, sender):
        return pltpu.make_async_remote_copy(
            src_ref=source(rank), dst_ref=slots.at[sender], send_sem=sends.at[rank], recv_sem=recvs.at[sender],
            device_id=device(rank), device_id_type=pl.DeviceIdType.MESH)

    def send(i, carry):
        parcel(lax.rem(me + i, count), me).start()
        return carry

    lax.fori_loop(1, count, send, 0)

    def settle(i, carry):
        other = lax.rem(me + i, count)
        parcel(other, other).wait()
        return carry

    lax.fori_loop(1, count, settle, 0)


def reduce_kernel(part_ref, conv_ref, cbias_ref, out_ref, obias_ref, split, first, piece, second, total, result,
                  s1, r1, s2, r2, s3, r3):
    greet(1, 1)
    me, mine = team_rank(), lax.axis_index("dp")
    for j in range(TEAM):
        split[j] = part_ref[PIECE * j:PIECE * (j + 1), :]
    first[me] = split[me]
    swap(None, first, s1, r1, TEAM, me, team_device, lambda rank: split.at[rank])
    piece[...] = jnp.sum(first[...], axis=0)
    second[mine] = piece[...]
    swap(None, second, s2, r2, DP, mine, lambda rank: {"dp": rank}, lambda rank: piece)
    total[...] = jnp.sum(second[...], axis=0)
    result[me] = total[...]
    swap(None, result, s3, r3, TEAM, me, team_device, lambda rank: total)
    for j in range(TEAM):
        lo = PIECE * j
        both = result[j]
        out_ref[lo:lo + PIECE, :] = both[:, HID:]
        if lo < FEATS:
            conv_ref[lo:lo + PIECE, :] = both[:, :HID]
        elif lo == FEATS:
            cbias_ref[...] = both[0:1, :HID]
            obias_ref[...] = both[1:2, :HID]


def reduce_grads(part):
    vm = pl.BlockSpec(memory_space=pltpu.VMEM)
    return pl.pallas_call(
        reduce_kernel,
        out_shape=(jax.ShapeDtypeStruct((FEATS, HID), F32), jax.ShapeDtypeStruct((1, HID), F32),
                   jax.ShapeDtypeStruct((HID, BINS), F32), jax.ShapeDtypeStruct((1, BINS), F32)),
        in_specs=[vm],
        out_specs=(vm, vm, vm, vm),
        scratch_shapes=[
            pltpu.VMEM((TEAM, PIECE, 128), F32), pltpu.VMEM((TEAM, PIECE, 128), F32), pltpu.VMEM((PIECE, 128), F32),
            pltpu.VMEM((DP, PIECE, 128), F32), pltpu.VMEM((PIECE, 128), F32), pltpu.VMEM((TEAM, PIECE, 128), F32),
            pltpu.SemaphoreType.DMA((TEAM,)), pltpu.SemaphoreType.DMA((TEAM,)),
            pltpu.SemaphoreType.DMA((DP,)), pltpu.SemaphoreType.DMA((DP,)),
            pltpu.SemaphoreType.DMA((TEAM,)), pltpu.SemaphoreType.DMA((TEAM,)),
        ],
        compiler_params=pltpu.CompilerParams(collective_id=1, has_side_effects=True),
        name="reduce_grads",
    )(part)


def shards(fraction, labels, conv_weight, conv_bias, out_weight, out_bias):
    patch = relay(fraction.reshape(fraction.shape[1:]))
    loss, part = compute(patch, labels.reshape(PX, PLANE), conv_weight, conv_bias, out_weight, out_bias, 1.0 / 25165824)
    conv, cbias, out, obias = reduce_grads(part)
    return loss.reshape(labels.shape), conv, cbias.reshape(HID), out, obias.reshape(BINS)


def solution(mesh):
    placed = (P("dp", None, "sp", "sec"), P("dp", ("sec", "sp"), None, None), P(), P(), P(), P())
    return jax.shard_map(
        shards,
        mesh=mesh,
        in_specs=placed,
        out_specs=(P("dp", ("sec", "sp"), None, None), P(), P(), P(), P()),
        check_vma=False,
    )
```

```python
import functools
import jax
import jax.numpy as jnp
from jax import lax
from jax.experimental import pallas as pl
from jax.experimental.pallas import tpu as pltpu
from jax.sharding import PartitionSpec as P

PX, PY, PZ = 32, 32, 32
PLANE = PY * PZ
HID = 64
BINS = 64
FEATS = 54
XB = 8
NB = PX // XB
GROUP = 24
KC = 9 * GROUP
KP = KC + 8
KO = HID + 16
TILE = 256
F32, BF16 = jnp.float32, jnp.bfloat16
LEAD = 3
CH = 2
NT = (((1,), (1,)), ((), ()))
TN = (((0,), (0,)), ((), ()))


def iota(shape, axis):
    return lax.broadcasted_iota(jnp.int32, shape, axis)


def split3(value):
    high = value.astype(BF16)
    rest = value - high.astype(F32)
    mid = rest.astype(BF16)
    low = (rest - mid.astype(F32)).astype(BF16)
    return high.astype(F32), mid.astype(F32), low.astype(F32)


def column(row):
    n = row.shape[1]
    eye = iota((n, n), 0) == iota((n, n), 1)
    return jnp.sum(jnp.where(eye, row, 0.0), axis=1, keepdims=True)


def conv_rows(p_minus_x, shape, k_axis, c_axis):
    col = iota(shape, c_axis)
    k = iota(shape, k_axis)
    t = col // GROUP
    u = col - t * GROUP
    c = jnp.where(u >= 10, 1, 0)
    dx = u - 10 * c - p_minus_x
    return (col < KC) & (u < 20) & (dx >= 0) & (dx < 3) & (k == 18 * dx + 2 * t + c)


def prepare(cw_ref, cb_ref, ow_ref, ob_ref, wide_ref, owt_ref, owb_ref):
    cb = column(cb_ref[...].reshape(1, HID)) * 0.5
    ch, cm, cl = split3(cb)
    col = iota((HID, KP), 1)
    bias = jnp.where(col == KC, ch, jnp.where(col == KC + 1, cm, jnp.where(col == KC + 2, cl, 0.0)))
    cw = cw_ref[...]
    for x in range(XB):
        pick = jnp.where(conv_rows(x, (FEATS, KP), 0, 1), 0.5, 0.0).astype(BF16)
        row = lax.dot_general(cw, pick, TN, preferred_element_type=F32) + bias
        wide_ref[x * HID:(x + 1) * HID, :] = row.astype(BF16)
    ob = column(ob_ref[...].reshape(1, BINS))
    oh, om, ol = split3(ob)
    ow = ow_ref[...]
    eye = (iota((HID, KO), 0) == iota((HID, KO), 1)).astype(F32).astype(BF16)
    owt = lax.dot_general(ow, eye, TN, preferred_element_type=F32)
    col = iota((BINS, KO), 1)
    owt = owt + jnp.where(col == HID, oh, jnp.where(col == HID + 1, om, jnp.where(col == HID + 2, ol, 0.0)))
    owt_ref[...] = owt.astype(BF16)
    owb_ref[...] = (ow.astype(F32) * 0.5).astype(BF16)


def box(padded_ref, square, z_lo, z_hi, y_lo, y_hi):
    a, b, c = padded_ref[7:39, :], padded_ref[8:40, :], padded_ref[9:41, :]
    if square:
        s = a * a + b * b + c * c
    else:
        s = a + b + c
    s = s + jnp.where(z_lo, 0.0, pltpu.roll(s, 1, 1)) + jnp.where(z_hi, 0.0, pltpu.roll(s, PLANE - 1, 1))
    s = s + jnp.where(y_lo, 0.0, pltpu.roll(s, PZ, 1)) + jnp.where(y_hi, 0.0, pltpu.roll(s, PLANE - PZ, 1))
    return s / 27.0


def edges(shape):
    pos = iota(shape, 1)
    z = pos & (PZ - 1)
    return z == 0, z == PZ - 1, pos < PZ, pos >= PLANE - PZ


def filter_patch(patch_ref, pad_ref, f0_ref, f1_ref):
    zero = jnp.zeros((8, PLANE), F32)
    for ref in (pad_ref, f0_ref, f1_ref):
        ref[0:8, :] = zero
        ref[40:48, :] = zero
    for i in range(8):
        pad_ref[8 + 4 * i:12 + 4 * i, :] = patch_ref[i]
    z_lo, z_hi, y_lo, y_hi = edges((PX, PLANE))
    filt = box(pad_ref, False, z_lo, z_hi, y_lo, y_hi)
    f0_ref[8:40, :] = filt
    f1_ref[8:40, :] = box(pad_ref, True, z_lo, z_hi, y_lo, y_hi) - filt * filt


def stencil(f0_ref, f1_ref, join_ref, g_ref):
    z_lo, z_hi, y_lo, y_hi = edges((GROUP, PLANE))
    join_ref[20:24, :] = jnp.zeros((4, PLANE), F32)
    for b in range(NB):
        join_ref[0:10, :] = f0_ref[8 * b + 7:8 * b + 17, :]
        join_ref[10:20, :] = f1_ref[8 * b + 7:8 * b + 17, :]
        mid = join_ref[...]
        lo = jnp.where(z_lo, 0.0, pltpu.roll(mid, 1, 1))
        hi = jnp.where(z_hi, 0.0, pltpu.roll(mid, PLANE - 1, 1))
        parts = []
        for step_y in (-1, 0, 1):
            for v in (lo, mid, hi):
                if step_y == -1:
                    v = jnp.where(y_lo, 0.0, pltpu.roll(v, PZ, 1))
                elif step_y == 1:
                    v = jnp.where(y_hi, 0.0, pltpu.roll(v, PLANE - PZ, 1))
                parts.append(v)
        parts.append(jnp.ones((8, PLANE), F32))
        g_ref[b] = jnp.concatenate(parts, axis=0).astype(BF16)


def fold(v):
    return v[:, :128] + v[:, 128:]


def train(labels_ref, wide_ref, owt_ref, owb_ref, g_ref, act_ref, d_ref, low_ref, grad_ref, z_ref, pick_ref, dconv_ref, dout_ref, hsum_ref, rsum_ref, scale):
    dconv_ref[...] = jnp.zeros_like(dconv_ref)
    dout_ref[...] = jnp.zeros_like(dout_ref)
    hsum_ref[...] = jnp.zeros_like(hsum_ref)
    rsum_ref[...] = jnp.zeros_like(rsum_ref)
    low_ref[...] = jnp.zeros_like(low_ref)
    grad_ref[...] = jnp.zeros_like(grad_ref)
    act_ref[...] = jnp.zeros_like(act_ref)
    bins = iota((BINS, TILE), 0)
    ones = jnp.ones((16, TILE), BF16)
    width = CH * TILE
    per = PLANE // width
    steps = NB * per

    def place(step, c):
        b = step // per
        return b, pl.ds(pl.multiple_of((step % per) * width + c * TILE, TILE), TILE)

    def whole(step):
        b = step // per
        return b, pl.ds(pl.multiple_of((step % per) * width, width), width)

    def ahead(step, slot, c):
        b, cols = place(step, c)
        u_all = jnp.dot(wide_ref[...], g_ref[b, :, cols], preferred_element_type=F32)
        for x in range(XB):
            u = u_all[x * HID:(x + 1) * HID]
            t = jnp.tanh(u)
            w = 1.0 + t
            a = u * w
            act_ref[slot, x, :, c * TILE:(c + 1) * TILE] = a.astype(BF16)
            d_ref[slot, x, :, c * TILE:(c + 1) * TILE] = (w + a) - a * t

    def behind_out(step, act_slot, slot):
        dout_ref[...] += lax.dot_general(
            jnp.concatenate([act_ref[act_slot, x] for x in range(XB)], axis=1),
            jnp.concatenate([low_ref[slot, x] for x in range(XB)], axis=1), NT, preferred_element_type=F32)

    def behind_conv(step, slot):
        b, cols = whole(step)
        dconv_ref[...] += lax.dot_general(grad_ref[slot], g_ref[b, :, cols], NT, preferred_element_type=F32)

    for c in range(CH):
        ahead(0, 0, c)

    def body(step, carry):
        slot = lax.rem(step, 2)
        slot3 = lax.rem(step, 3)
        next3 = lax.rem(step + 1, 3)
        last3 = lax.rem(step + 2, 3)
        last = jnp.maximum(step - 1, 0)

        def project(c, x):
            return jnp.dot(owt_ref[...], jnp.concatenate([act_ref[slot3, x, :, c * TILE:(c + 1) * TILE], ones], axis=0), preferred_element_type=F32)

        tiles = [(c, x) for c in range(CH) for x in range(XB)]
        count = len(tiles)
        logits_of = {i: project(*tiles[i]) for i in range(LEAD)}
        backs = {}
        hsum = rsum = None
        for i in range(count + 1):
            if i < count:
                c, x = tiles[i]
                span = slice(c * TILE, (c + 1) * TILE)
                b, cols = place(step, c)
                logits = logits_of.pop(i)
                if i + LEAD < count:
                    logits_of[i + LEAD] = project(*tiles[i + LEAD])
                if i % XB == 0:
                    ahead_at(ahead, step, next3, c, steps)
                e = jnp.exp(logits)
                row = XB * b + x
                hit = bins == labels_ref[pl.ds(row, 1), cols]
                total = jnp.sum(e, axis=0, keepdims=True)
                z_ref[pl.ds(row, 1), cols] = total
                pick_ref[pl.ds(row, 1), cols] = jnp.sum(jnp.where(hit, logits, 0.0), axis=0, keepdims=True)
                r = e * (scale / total) - jnp.where(hit, scale, 0.0)
                low = r.astype(BF16)
                low_ref[slot, x, :, span] = low
                rsum = fold(r) if rsum is None else rsum + fold(r)
                backs[i] = jnp.dot(owb_ref[...], low, preferred_element_type=F32)
                if i == count // 4:
                    behind_out(last, last3, 1 - slot)
                if i == count // 2:
                    behind_conv(last, 1 - slot)
            if i >= 1:
                c, x = tiles[i - 1]
                span = slice(c * TILE, (c + 1) * TILE)
                grad = backs.pop(i - 1) * d_ref[slot3, x, :, span]
                grad_ref[slot, x * HID:(x + 1) * HID, span] = grad.astype(BF16)
                hsum = fold(grad) if hsum is None else hsum + fold(grad)
        hsum_ref[...] += hsum
        rsum_ref[...] += rsum
        return carry

    lax.fori_loop(0, steps, body, 0)
    behind_out(steps - 1, (steps - 1) % 3, (steps - 1) % 2)
    behind_conv(steps - 1, (steps - 1) % 2)


def ahead_at(ahead, step, slot, c, steps):
    ahead(jnp.minimum(step + 1, steps - 1), slot, c)


def finish(dconv_ref, dout_ref, hsum_ref, rsum_ref, part_ref):
    total = dconv_ref[0:HID, :]
    for x in range(1, XB):
        total = total + pltpu.roll(dconv_ref[x * HID:(x + 1) * HID, :], KP - x, 1)
    col = iota((HID, KP), 1)
    hcol = jnp.sum(hsum_ref[...], axis=1, keepdims=True)
    rcol = jnp.sum(rsum_ref[...], axis=1, keepdims=True)
    total = jnp.where(col == KC, hcol, jnp.where(col == KC + 1, rcol, total))
    k, c = iota((HID, KP), 0), iota((HID, KP), 1)
    pick = conv_rows(0, (HID, KP), 0, 1) | ((k == FEATS) & (c == KC)) | ((k == FEATS + 1) & (c == KC + 1))
    rows = lax.dot_general(jnp.where(pick, 1.0, 0.0), total, NT, precision=lax.Precision.HIGHEST, preferred_element_type=F32)
    part_ref[:, 0:HID] = rows
    part_ref[:, HID:2 * HID] = dout_ref[...]


def compute_scratch():
    return [
        pltpu.VMEM((48, PLANE), F32), pltpu.VMEM((48, PLANE), F32), pltpu.VMEM((48, PLANE), F32),
        pltpu.VMEM((GROUP, PLANE), F32),
        pltpu.VMEM((NB, KP, PLANE), BF16),
        pltpu.VMEM((XB * HID, KP), BF16), pltpu.VMEM((BINS, KO), BF16), pltpu.VMEM((HID, BINS), BF16),
        pltpu.VMEM((3, XB, HID, CH * TILE), BF16), pltpu.VMEM((3, XB, HID, CH * TILE), F32),
        pltpu.VMEM((2, XB, BINS, CH * TILE), BF16), pltpu.VMEM((2, XB * HID, CH * TILE), BF16),
        pltpu.VMEM((XB * HID, KP), F32), pltpu.VMEM((HID, BINS), F32),
        pltpu.VMEM((HID, 128), F32), pltpu.VMEM((BINS, 128), F32),
    ]


SEC, SP, YHI, Z = 4, 8, 2, 12
TEAM = SEC * SP
Y = SEC * YHI
ROWS = HID // SP
SCALE = 1.0 / 25165824
MESH = pl.DeviceIdType.MESH


def place_here():
    sec, sp, dp = lax.axis_index("sec"), lax.axis_index("sp"), lax.axis_index("dp")
    return sec, sp, dp // Z, lax.rem(dp, Z)


def team_device(rank):
    return {"sec": rank // SP, "sp": lax.rem(rank, SP)}


def greet():
    barrier = pltpu.get_barrier_semaphore()
    sec, sp, yhi, z = place_here()
    me = sec * SP + sp

    def hail(device):
        pl.semaphore_signal(barrier, inc=1, device_id=device, device_id_type=MESH)

    def along_z(i, carry):
        hail({"dp": yhi * Z + lax.rem(z + i, Z)})
        return carry

    def along_y(i, carry):
        hail({"sec": i, "dp": (1 - yhi) * Z + z})
        return carry

    def in_team(i, carry):
        hail(team_device(lax.rem(me + i, TEAM)))
        return carry

    lax.fori_loop(1, Z, along_z, 0)
    lax.fori_loop(0, SEC, along_y, 0)
    lax.fori_loop(1, TEAM, in_team, 0)
    pl.semaphore_wait(barrier, Z - 1 + SEC + TEAM - 1)


def relay(frac_ref, patch_ref, own_sem, send_sems, recv_sems):
    sec, sp, _, _ = place_here()
    me = sec * SP + sp
    spot = patch_ref.at[sp, :, pl.ds(pl.multiple_of(sec * (PLANE // SEC), PLANE // SEC), PLANE // SEC)]

    def parcel(rank, sender):
        return pltpu.make_async_remote_copy(
            src_ref=frac_ref.at[rank], dst_ref=spot, send_sem=send_sems.at[rank], recv_sem=recv_sems.at[sender],
            device_id=team_device(rank), device_id_type=MESH)

    def send(i, carry):
        a, b = i // SP, lax.rem(i, SP)
        far = jnp.where(sec < SEC // 2, SEC - 1 - a, a)
        chip = lax.rem(sp // 2 + 2 + 3 * (b // 2), SP // 2)
        rank = far * SP + chip * 2 + lax.rem(sp + b, 2)

        @pl.when(rank != me)
        def _():
            parcel(rank, me).start()

        return carry

    lax.fori_loop(0, TEAM, send, 0)
    own = pltpu.make_async_copy(frac_ref.at[me], spot, own_sem)
    own.start()

    def arrive():
        def take(i, carry):
            other = lax.rem(me + i, TEAM)
            parcel(other, other).wait_recv()
            return carry

        lax.fori_loop(1, TEAM, take, 0)
        own.wait()

    def leave():
        def drop(i, carry):
            other = lax.rem(me + i, TEAM)
            parcel(other, other).wait_send()
            return carry

        lax.fori_loop(1, TEAM, drop, 0)

    return arrive, leave


def swap(count, me, device, source, slots, sends, recvs, meanwhile=None):
    def parcel(rank, sender):
        return pltpu.make_async_remote_copy(
            src_ref=source(rank), dst_ref=slots.at[sender], send_sem=sends.at[rank], recv_sem=recvs.at[sender],
            device_id=device(rank), device_id_type=MESH)

    def send(i, carry):
        parcel(lax.rem(me + i, count), me).start()
        return carry

    def take(i, carry):
        other = lax.rem(me + i, count)
        parcel(other, other).wait_recv()
        return carry

    def leave():
        def drop(i, carry):
            other = lax.rem(me + i, count)
            parcel(other, other).wait_send()
            return carry

        lax.fori_loop(1, count, drop, 0)

    lax.fori_loop(1, count, send, 0)
    if meanwhile is not None:
        meanwhile()
    lax.fori_loop(1, count, take, 0)
    return leave


def reduce_grads(meanwhile, part, first, second, third, result, piece, piece2, total, s1, r1, s2, r2, s3, r3, s4, r4):
    sec, sp, yhi, z = place_here()

    def rows(rank):
        return part.at[pl.ds(pl.multiple_of(rank * ROWS, ROWS), ROWS), :]

    def own_chip(rank):
        return {"sp": rank}

    leaves = []
    first[sp] = rows(sp)[...]
    leaves.append(swap(SP, sp, own_chip, rows, first, s1, r1))
    piece[...] = jnp.sum(first[...], axis=0)
    y = yhi * SEC + sec
    second[y] = piece[...]
    leaves.append(swap(Y, y, lambda rank: {"sec": lax.rem(rank, SEC), "dp": rank // SEC * Z + z}, lambda rank: piece, second, s2, r2))
    piece2[...] = jnp.sum(second[...], axis=0)
    third[z] = piece2[...]
    leaves.append(swap(Z, z, lambda rank: {"dp": yhi * Z + rank}, lambda rank: piece2, third, s3, r3, meanwhile))
    total[...] = jnp.sum(third[...], axis=0)
    result[sp] = total[...]
    leaves.append(swap(SP, sp, own_chip, lambda rank: total, result, s4, r4))
    return leaves


def step_kernel(frac_ref, labels_ref, cw_ref, cb_ref, ow_ref, ob_ref, grads_ref, loss_ref,
                z, pick, loss, out_sems, patch, labels, cw, cb, ow, ob, in_sems, own_sem, send_sems, recv_sems,
                part, first, second, third, result, piece, piece2, total, s1, r1, s2, r2, s3, r3, s4, r4,
                pad, f0, f1, join, g, wide, owt, owb, act, d, low, grad, dconv, dout, hsum, rsum):
    loads = [pltpu.make_async_copy(src, dst, in_sems.at[i]) for i, (src, dst) in enumerate(
        ((cw_ref, cw), (cb_ref, cb), (ow_ref, ow), (ob_ref, ob), (labels_ref, labels)))]
    for load in loads:
        load.start()
    greet()
    arrive, leave = relay(frac_ref, patch, own_sem, send_sems, recv_sems)
    for load in loads:
        load.wait()
    prepare(cw, cb, ow, ob, wide, owt, owb)
    arrive()
    filter_patch(patch, pad, f0, f1)
    stencil(f0, f1, join, g)
    train(labels, wide, owt, owb, g, act, d, low, grad, z, pick, dconv, dout, hsum, rsum, SCALE)
    finish(dconv, dout, hsum, rsum, part)

    def save_loss():
        loss[...] = jnp.log(z[...]) - pick[...]
        pltpu.make_async_copy(loss, loss_ref, out_sems.at[0]).start()

    leaves = reduce_grads(save_loss, part, first, second, third, result, piece, piece2, total, s1, r1, s2, r2, s3, r3, s4, r4)
    save = pltpu.make_async_copy(result, grads_ref, out_sems.at[1])
    save.start()
    for end in [leave] + leaves:
        end()
    pltpu.make_async_copy(loss, loss_ref, out_sems.at[0]).wait()
    save.wait()


def train_step(frac, labels, cw, cb, ow, ob):
    far = pl.BlockSpec(memory_space=pl.ANY)
    dma = pltpu.SemaphoreType.DMA
    tile = pltpu.VMEM((ROWS, 128), F32)
    plane = pltpu.VMEM((PX, PLANE), F32)
    return pl.pallas_call(
        step_kernel,
        out_shape=(jax.ShapeDtypeStruct((SP, ROWS, 128), F32), jax.ShapeDtypeStruct((PX, PLANE), F32)),
        in_specs=[far] * 6,
        out_specs=(far, far),
        scratch_shapes=[
            plane, plane, plane, dma((2,)),
            pltpu.VMEM((SP, PX // SP, PLANE), F32), pltpu.VMEM((PX, PLANE), jnp.int32),
            pltpu.VMEM((FEATS, HID), BF16), pltpu.VMEM((HID,), F32), pltpu.VMEM((HID, BINS), BF16), pltpu.VMEM((BINS,), F32),
            dma((5,)), dma, dma((TEAM,)), dma((TEAM,)),
            pltpu.VMEM((HID, 128), F32), pltpu.VMEM((SP, ROWS, 128), F32), pltpu.VMEM((Y, ROWS, 128), F32),
            pltpu.VMEM((Z, ROWS, 128), F32), pltpu.VMEM((SP, ROWS, 128), F32), tile, tile, tile,
            dma((SP,)), dma((SP,)), dma((Y,)), dma((Y,)), dma((Z,)), dma((Z,)), dma((SP,)), dma((SP,)),
        ] + compute_scratch(),
        compiler_params=pltpu.CompilerParams(collective_id=0, has_side_effects=True, vmem_limit_bytes=56 * 2**20),
        name="train_step",
    )(frac, labels, cw, cb, ow, ob)


def close_kernel(grads_ref, loss_in, loss_ref, conv_ref, cbias_ref, out_ref, obias_ref, grads, sems):
    loss = pltpu.make_async_copy(loss_in, loss_ref, sems.at[0])
    load = pltpu.make_async_copy(grads_ref, grads, sems.at[1])
    load.start()
    loss.start()
    load.wait()
    full = jnp.concatenate([grads[i] for i in range(SP)], axis=0)
    conv_ref[...] = full[:FEATS, :HID]
    cbias_ref[...] = full[FEATS:FEATS + 1, :HID].reshape(HID)
    obias_ref[...] = full[FEATS + 1:FEATS + 2, :HID].reshape(BINS)
    out_ref[...] = full[:, HID:]
    loss.wait()


def close(grads, loss):
    vm, far = pl.BlockSpec(memory_space=pltpu.VMEM), pl.BlockSpec(memory_space=pl.ANY)
    return pl.pallas_call(
        close_kernel,
        out_shape=(jax.ShapeDtypeStruct((PX, PLANE), F32), jax.ShapeDtypeStruct((FEATS, HID), F32),
                   jax.ShapeDtypeStruct((HID,), F32), jax.ShapeDtypeStruct((HID, BINS), F32),
                   jax.ShapeDtypeStruct((BINS,), F32)),
        in_specs=[far, far],
        out_specs=(far, vm, vm, vm, vm),
        scratch_shapes=[pltpu.VMEM((SP, ROWS, 128), F32), pltpu.SemaphoreType.DMA((2,))],
        compiler_params=pltpu.CompilerParams(vmem_limit_bytes=56 * 2**20),
        name="close_step",
    )(grads, loss)


def shards(fraction, labels, conv_weight, conv_bias, out_weight, out_bias):
    grads, loss = train_step(fraction.reshape(fraction.shape[1:]), labels.reshape(PX, PLANE),
                             conv_weight, conv_bias, out_weight, out_bias)
    loss, conv, cbias, out, obias = close(grads, loss)
    return loss.reshape(labels.shape), conv, cbias, out, obias


def solution(mesh):
    placed = (P("dp", None, "sp", "sec"), P("dp", ("sec", "sp"), None, None), P(), P(), P(), P())
    return jax.shard_map(
        shards,
        mesh=mesh,
        in_specs=placed,
        out_specs=(P("dp", ("sec", "sp"), None, None), P(), P(), P(), P()),
        check_vma=False,
    )
```

```python
import functools
import jax
import jax.numpy as jnp
from jax import lax
from jax.experimental import pallas as pl
from jax.experimental.pallas import tpu as pltpu
from jax.sharding import PartitionSpec as P

PX, PY, PZ = 32, 32, 32
PLANE = PY * PZ
HID = 64
BINS = 64
FEATS = 54
XB = 8
NB = PX // XB
GROUP = 24
KC = 9 * GROUP
KP = KC + 8
KO = HID + 16
TILE = 256
F32, BF16 = jnp.float32, jnp.bfloat16
LEAD = 2
CH = 2
HIDDEN_AT = (0, 6)
CONV_AT = (1, 3)
OUT_AT = (5, 7, 9, 11)
NT = (((1,), (1,)), ((), ()))
TN = (((0,), (0,)), ((), ()))


def iota(shape, axis):
    return lax.broadcasted_iota(jnp.int32, shape, axis)


def split3(value):
    high = value.astype(BF16)
    rest = value - high.astype(F32)
    mid = rest.astype(BF16)
    low = (rest - mid.astype(F32)).astype(BF16)
    return high.astype(F32), mid.astype(F32), low.astype(F32)


def column(row):
    n = row.shape[1]
    eye = iota((n, n), 0) == iota((n, n), 1)
    return jnp.sum(jnp.where(eye, row, 0.0), axis=1, keepdims=True)


def conv_rows(p_minus_x, shape, k_axis, c_axis):
    col = iota(shape, c_axis)
    k = iota(shape, k_axis)
    t = col // GROUP
    u = col - t * GROUP
    c = jnp.where(u >= 10, 1, 0)
    dx = u - 10 * c - p_minus_x
    return (col < KC) & (u < 20) & (dx >= 0) & (dx < 3) & (k == 18 * dx + 2 * t + c)


def prepare(cw_ref, cb_ref, ow_ref, ob_ref, wide_ref, owt_ref, owb_ref):
    cb = column(cb_ref[...].reshape(1, HID)) * 0.5
    ch, cm, cl = split3(cb)
    col = iota((HID, KP), 1)
    bias = jnp.where(col == KC, ch, jnp.where(col == KC + 1, cm, jnp.where(col == KC + 2, cl, 0.0)))
    cw = cw_ref[...]
    for x in range(XB):
        pick = jnp.where(conv_rows(x, (FEATS, KP), 0, 1), 0.5, 0.0).astype(BF16)
        row = lax.dot_general(cw, pick, TN, preferred_element_type=F32) + bias
        wide_ref[x * HID:(x + 1) * HID, :] = row.astype(BF16)
    ob = column(ob_ref[...].reshape(1, BINS))
    oh, om, ol = split3(ob)
    ow = ow_ref[...]
    eye = (iota((HID, KO), 0) == iota((HID, KO), 1)).astype(F32).astype(BF16)
    owt = lax.dot_general(ow, eye, TN, preferred_element_type=F32)
    col = iota((BINS, KO), 1)
    owt = owt + jnp.where(col == HID, oh, jnp.where(col == HID + 1, om, jnp.where(col == HID + 2, ol, 0.0)))
    owt_ref[...] = owt.astype(BF16)
    owb_ref[...] = (ow.astype(F32) * 0.5).astype(BF16)


def box(padded_ref, square, z_lo, z_hi, y_lo, y_hi):
    a, b, c = padded_ref[7:39, :], padded_ref[8:40, :], padded_ref[9:41, :]
    if square:
        s = a * a + b * b + c * c
    else:
        s = a + b + c
    s = s + jnp.where(z_lo, 0.0, pltpu.roll(s, 1, 1)) + jnp.where(z_hi, 0.0, pltpu.roll(s, PLANE - 1, 1))
    s = s + jnp.where(y_lo, 0.0, pltpu.roll(s, PZ, 1)) + jnp.where(y_hi, 0.0, pltpu.roll(s, PLANE - PZ, 1))
    return s / 27.0


def edges(shape):
    pos = iota(shape, 1)
    z = pos & (PZ - 1)
    return z == 0, z == PZ - 1, pos < PZ, pos >= PLANE - PZ


def filter_patch(patch_ref, pad_ref, f0_ref, f1_ref):
    zero = jnp.zeros((8, PLANE), F32)
    for ref in (pad_ref, f0_ref, f1_ref):
        ref[0:8, :] = zero
        ref[40:48, :] = zero
    for i in range(8):
        pad_ref[8 + 4 * i:12 + 4 * i, :] = patch_ref[i]
    z_lo, z_hi, y_lo, y_hi = edges((PX, PLANE))
    filt = box(pad_ref, False, z_lo, z_hi, y_lo, y_hi)
    f0_ref[8:40, :] = filt
    f1_ref[8:40, :] = box(pad_ref, True, z_lo, z_hi, y_lo, y_hi) - filt * filt


def stencil(f0_ref, f1_ref, join_ref, g_ref):
    z_lo, z_hi, y_lo, y_hi = edges((GROUP, PLANE))
    join_ref[20:24, :] = jnp.zeros((4, PLANE), F32)
    for b in range(NB):
        join_ref[0:10, :] = f0_ref[8 * b + 7:8 * b + 17, :]
        join_ref[10:20, :] = f1_ref[8 * b + 7:8 * b + 17, :]
        mid = join_ref[...]
        lo = jnp.where(z_lo, 0.0, pltpu.roll(mid, 1, 1))
        hi = jnp.where(z_hi, 0.0, pltpu.roll(mid, PLANE - 1, 1))
        parts = []
        for step_y in (-1, 0, 1):
            for v in (lo, mid, hi):
                if step_y == -1:
                    v = jnp.where(y_lo, 0.0, pltpu.roll(v, PZ, 1))
                elif step_y == 1:
                    v = jnp.where(y_hi, 0.0, pltpu.roll(v, PLANE - PZ, 1))
                parts.append(v)
        parts.append(jnp.ones((8, PLANE), F32))
        g_ref[b] = jnp.concatenate(parts, axis=0).astype(BF16)


def fold(v):
    return v[:, :128] + v[:, 128:]


def train(labels_ref, bins_ref, early_ref, wide_ref, owt_ref, owb_ref, g_ref, act_ref, d_ref, low_ref, grad_ref, z_ref, pick_ref, dconv_ref, dout_ref, hsum_ref, rsum_ref, scale):
    for ref in (dconv_ref, dout_ref, hsum_ref, rsum_ref, low_ref, grad_ref, act_ref, d_ref):
        ref[...] = jnp.zeros_like(ref)
    bins_ref[...] = iota((BINS, TILE), 0)
    ones = jnp.ones((16, TILE), BF16)
    width = CH * TILE
    per = PLANE // width
    steps = NB * per
    tiles = [(c, x) for c in range(CH) for x in range(XB)]

    def span(c):
        return slice(c * TILE, (c + 1) * TILE)

    def place(step, c):
        return step // per, pl.ds(pl.multiple_of((step % per) * width + c * TILE, TILE), TILE)

    def within(step):
        return jnp.clip(step, 0, steps - 1)

    def hidden_dot(step, c):
        b, cols = place(within(step), c)
        return jnp.dot(wide_ref[...], g_ref[b, :, cols], preferred_element_type=F32)

    def silu(step, c, x, u_all):
        slot = lax.rem(step, 3)
        u = u_all[x * HID:(x + 1) * HID]
        t = jnp.tanh(u)
        w = 1.0 + t
        a = u * w
        act_ref[slot, x, :, span(c)] = a.astype(BF16)
        d_ref[slot, x, :, span(c)] = (w + a) - a * t

    def hidden(step):
        for c in range(CH):
            u_all = hidden_dot(step, c)
            for x in range(XB):
                silu(step, c, x, u_all)

    def logit(step, c, x):
        slot = lax.rem(step, 3)
        return jnp.dot(owt_ref[...], jnp.concatenate([act_ref[slot, x, :, span(c)], ones], axis=0), preferred_element_type=F32)

    def softmax(step, c, x, logits):
        b, cols = place(step, c)
        row = XB * b + x
        e = jnp.exp(logits)
        hot = jnp.where(bins_ref[...] == labels_ref[pl.ds(row, 1), cols], scale, 0.0)
        picked = logits * hot
        picked = sum(picked[8 * k:8 * k + 8] for k in range(BINS // 8))
        for half in range(TILE // 128):
            lane = (step % per) * (width // 128) + c * (TILE // 128) + half
            pick_ref[lane, pl.ds(pl.multiple_of(8 * row, 8), 8), :] = picked[:, 128 * half:128 * half + 128]
        total = jnp.sum(e, axis=0, keepdims=True)
        z_ref[pl.ds(row, 1), cols] = total
        r = e * (scale / total) - hot
        low_ref[lax.rem(step, 2), x, :, span(c)] = r.astype(BF16)
        return fold(r)

    def back(step, c, x):
        prod = jnp.dot(owb_ref[...], low_ref[lax.rem(step, 2), x, :, span(c)], preferred_element_type=F32)
        grad = prod * d_ref[lax.rem(step, 3), x, :, span(c)]
        grad_ref[lax.rem(step, 2), x * HID:(x + 1) * HID, span(c)] = grad.astype(BF16)
        return fold(grad)

    def out_grad(step, part, parts):
        xs = range(part * XB // parts, (part + 1) * XB // parts)
        dout_ref[...] += lax.dot_general(
            jnp.concatenate([act_ref[lax.rem(step, 3), x] for x in xs], axis=1),
            jnp.concatenate([low_ref[lax.rem(step, 2), x] for x in xs], axis=1), NT, preferred_element_type=F32)

    def conv_grad(step, at, part, parts):
        b = at // per
        cols = pl.ds(pl.multiple_of((at % per) * width, width), width)
        rows = slice(part * XB * HID // parts, (part + 1) * XB * HID // parts)
        dconv_ref[rows, :] += lax.dot_general(grad_ref[lax.rem(step, 2), rows, :], g_ref[b, :, cols], NT, preferred_element_type=F32)

    def add(total, term):
        return term if total is None else total + term

    hidden(0)
    for i in range(LEAD):
        early_ref[i] = logit(0, *tiles[i])

    def body(step, carry):
        old, oldest, ahead = step + 5, step + 4, step + 1
        hsum = rsum = None
        logits = {t: early_ref[i] for i, t in enumerate(tiles[:LEAD])}
        n = len(tiles)
        u_all = {}
        for i, t in enumerate(tiles):
            if i in HIDDEN_AT:
                u_all[HIDDEN_AT.index(i)] = hidden_dot(ahead, HIDDEN_AT.index(i))
            if i + LEAD < n:
                logits[tiles[i + LEAD]] = logit(step, *tiles[i + LEAD])
            if i in CONV_AT:
                conv_grad(oldest, within(step - 2), CONV_AT.index(i), len(CONV_AT))
            if i in OUT_AT:
                out_grad(old, OUT_AT.index(i), len(OUT_AT))
            hsum = add(hsum, back(old, *t))
            silu(ahead, *t, u_all[t[0]])
            rsum = add(rsum, softmax(step, *t, logits.pop(t)))
        for i in range(LEAD):
            early_ref[i] = logit(ahead, *tiles[i])
        rsum_ref[...] += rsum
        hsum_ref[...] += hsum
        return carry

    lax.fori_loop(0, steps, body, 0)
    hsum = None
    for t in tiles:
        hsum = add(hsum, back(steps - 1, *t))
    hsum_ref[...] += hsum
    conv_grad(steps - 2, steps - 2, 0, 1)
    out_grad(steps - 1, 0, 1)
    conv_grad(steps - 1, steps - 1, 0, 1)


def losses(z_ref, pick_ref, loss_ref, scale):
    for lane in range(PLANE // 128):
        cols = slice(128 * lane, 128 * lane + 128)
        picked = sum(pick_ref[lane, pl.ds(k, PX, stride=8), :] for k in range(8))
        loss_ref[:, cols] = jnp.log(z_ref[:, cols]) - picked / scale


def finish(dconv_ref, dout_ref, hsum_ref, rsum_ref, part_ref):
    total = dconv_ref[0:HID, :]
    for x in range(1, XB):
        total = total + pltpu.roll(dconv_ref[x * HID:(x + 1) * HID, :], KP - x, 1)
    col = iota((HID, KP), 1)
    hcol = jnp.sum(hsum_ref[...], axis=1, keepdims=True)
    rcol = jnp.sum(rsum_ref[...], axis=1, keepdims=True)
    total = jnp.where(col == KC, hcol, jnp.where(col == KC + 1, rcol, total))
    k, c = iota((HID, KP), 0), iota((HID, KP), 1)
    pick = conv_rows(0, (HID, KP), 0, 1) | ((k == FEATS) & (c == KC)) | ((k == FEATS + 1) & (c == KC + 1))
    rows = lax.dot_general(jnp.where(pick, 1.0, 0.0), total, NT, precision=lax.Precision.HIGHEST, preferred_element_type=F32)
    part_ref[:, 0:HID] = rows
    part_ref[:, HID:2 * HID] = dout_ref[...]


def compute_scratch():
    return [
        pltpu.VMEM((48, PLANE), F32), pltpu.VMEM((48, PLANE), F32), pltpu.VMEM((48, PLANE), F32),
        pltpu.VMEM((GROUP, PLANE), F32),
        pltpu.VMEM((NB, KP, PLANE), BF16),
        pltpu.VMEM((XB * HID, KP), BF16), pltpu.VMEM((BINS, KO), BF16), pltpu.VMEM((HID, BINS), BF16),
        pltpu.VMEM((3, XB, HID, CH * TILE), BF16), pltpu.VMEM((3, XB, HID, CH * TILE), F32),
        pltpu.VMEM((2, XB, BINS, CH * TILE), BF16), pltpu.VMEM((2, XB * HID, CH * TILE), BF16), pltpu.VMEM((BINS, TILE), jnp.int32), pltpu.VMEM((LEAD, BINS, TILE), F32),
        pltpu.VMEM((XB * HID, KP), F32), pltpu.VMEM((HID, BINS), F32),
        pltpu.VMEM((HID, 128), F32), pltpu.VMEM((BINS, 128), F32),
    ]


SEC, SP, YHI, Z = 4, 8, 2, 12
TEAM = SEC * SP
Y = SEC * YHI
ROWS = HID // SP
SCALE = 1.0 / 25165824
MESH = pl.DeviceIdType.MESH


def place_here():
    sec, sp, dp = lax.axis_index("sec"), lax.axis_index("sp"), lax.axis_index("dp")
    return sec, sp, dp // Z, lax.rem(dp, Z)


def team_device(rank):
    return {"sec": rank // SP, "sp": lax.rem(rank, SP)}


def greet():
    barrier = pltpu.get_barrier_semaphore()
    sec, sp, yhi, z = place_here()
    me = sec * SP + sp

    def hail(device):
        pl.semaphore_signal(barrier, inc=1, device_id=device, device_id_type=MESH)

    def along_z(i, carry):
        hail({"dp": yhi * Z + lax.rem(z + i, Z)})
        return carry

    def along_y(i, carry):
        hail({"sec": i, "dp": (1 - yhi) * Z + z})
        return carry

    def in_team(i, carry):
        hail(team_device(lax.rem(me + i, TEAM)))
        return carry

    lax.fori_loop(1, Z, along_z, 0)
    lax.fori_loop(0, SEC, along_y, 0)
    lax.fori_loop(1, TEAM, in_team, 0)
    pl.semaphore_wait(barrier, Z - 1 + SEC + TEAM - 1)


def relay(frac_ref, patch_ref, own_sem, send_sems, recv_sems):
    sec, sp, _, _ = place_here()
    me = sec * SP + sp
    spot = patch_ref.at[sp, :, pl.ds(pl.multiple_of(sec * (PLANE // SEC), PLANE // SEC), PLANE // SEC)]

    def parcel(rank, sender):
        return pltpu.make_async_remote_copy(
            src_ref=frac_ref.at[rank], dst_ref=spot, send_sem=send_sems.at[rank], recv_sem=recv_sems.at[sender],
            device_id=team_device(rank), device_id_type=MESH)

    def send(i, carry):
        a, b = i // SP, lax.rem(i, SP)
        far = jnp.where(sec < SEC // 2, SEC - 1 - a, a)
        chip = lax.rem(sp // 2 + 2 + 3 * (b // 2), SP // 2)
        rank = far * SP + chip * 2 + lax.rem(sp + b, 2)

        @pl.when(rank != me)
        def _():
            parcel(rank, me).start()

        return carry

    lax.fori_loop(0, TEAM, send, 0)
    own = pltpu.make_async_copy(frac_ref.at[me], spot, own_sem)
    own.start()

    def arrive():
        def take(i, carry):
            other = lax.rem(me + i, TEAM)
            parcel(other, other).wait_recv()
            return carry

        lax.fori_loop(1, TEAM, take, 0)
        own.wait()

    def leave():
        def drop(i, carry):
            other = lax.rem(me + i, TEAM)
            parcel(other, other).wait_send()
            return carry

        lax.fori_loop(1, TEAM, drop, 0)

    return arrive, leave


def swap(count, me, device, source, slots, sends, recvs, meanwhile=None):
    def parcel(rank, sender):
        return pltpu.make_async_remote_copy(
            src_ref=source(rank), dst_ref=slots.at[sender], send_sem=sends.at[rank], recv_sem=recvs.at[sender],
            device_id=device(rank), device_id_type=MESH)

    def send(i, carry):
        parcel(lax.rem(me + i, count), me).start()
        return carry

    def take(i, carry):
        other = lax.rem(me + i, count)
        parcel(other, other).wait_recv()
        return carry

    def leave():
        def drop(i, carry):
            other = lax.rem(me + i, count)
            parcel(other, other).wait_send()
            return carry

        lax.fori_loop(1, count, drop, 0)

    lax.fori_loop(1, count, send, 0)
    if meanwhile is not None:
        meanwhile()
    lax.fori_loop(1, count, take, 0)
    return leave


def reduce_grads(meanwhile, part, first, second, third, result, piece, piece2, total, s1, r1, s2, r2, s3, r3, s4, r4):
    sec, sp, yhi, z = place_here()

    def rows(rank):
        return part.at[pl.ds(pl.multiple_of(rank * ROWS, ROWS), ROWS), :]

    def own_chip(rank):
        return {"sp": rank}

    leaves = []
    first[sp] = rows(sp)[...]
    leaves.append(swap(SP, sp, own_chip, rows, first, s1, r1))
    piece[...] = jnp.sum(first[...], axis=0)
    y = yhi * SEC + sec
    second[y] = piece[...]
    leaves.append(swap(Y, y, lambda rank: {"sec": lax.rem(rank, SEC), "dp": rank // SEC * Z + z}, lambda rank: piece, second, s2, r2))
    piece2[...] = jnp.sum(second[...], axis=0)
    third[z] = piece2[...]
    leaves.append(swap(Z, z, lambda rank: {"dp": yhi * Z + rank}, lambda rank: piece2, third, s3, r3, meanwhile))
    total[...] = jnp.sum(third[...], axis=0)
    result[sp] = total[...]
    leaves.append(swap(SP, sp, own_chip, lambda rank: total, result, s4, r4))
    return leaves


def step_kernel(frac_ref, labels_ref, cw_ref, cb_ref, ow_ref, ob_ref, grads_ref, loss_ref,
                z, pick, loss, out_sems, patch, labels, cw, cb, ow, ob, in_sems, own_sem, send_sems, recv_sems,
                part, first, second, third, result, piece, piece2, total, s1, r1, s2, r2, s3, r3, s4, r4,
                pad, f0, f1, join, g, wide, owt, owb, act, d, low, grad, bins, early, dconv, dout, hsum, rsum):
    loads = [pltpu.make_async_copy(src, dst, in_sems.at[i]) for i, (src, dst) in enumerate(
        ((cw_ref, cw), (cb_ref, cb), (ow_ref, ow), (ob_ref, ob), (labels_ref, labels)))]
    for load in loads:
        load.start()
    greet()
    arrive, leave = relay(frac_ref, patch, own_sem, send_sems, recv_sems)
    for load in loads:
        load.wait()
    prepare(cw, cb, ow, ob, wide, owt, owb)
    arrive()
    filter_patch(patch, pad, f0, f1)
    stencil(f0, f1, join, g)
    train(labels, bins, early, wide, owt, owb, g, act, d, low, grad, z, pick, dconv, dout, hsum, rsum, SCALE)
    finish(dconv, dout, hsum, rsum, part)

    def save_loss():
        losses(z, pick, loss, SCALE)
        pltpu.make_async_copy(loss, loss_ref, out_sems.at[0]).start()

    leaves = reduce_grads(save_loss, part, first, second, third, result, piece, piece2, total, s1, r1, s2, r2, s3, r3, s4, r4)
    save = pltpu.make_async_copy(result, grads_ref, out_sems.at[1])
    save.start()
    for end in [leave] + leaves:
        end()
    pltpu.make_async_copy(loss, loss_ref, out_sems.at[0]).wait()
    save.wait()


def train_step(frac, labels, cw, cb, ow, ob):
    far = pl.BlockSpec(memory_space=pl.ANY)
    dma = pltpu.SemaphoreType.DMA
    tile = pltpu.VMEM((ROWS, 128), F32)
    plane = pltpu.VMEM((PX, PLANE), F32)
    return pl.pallas_call(
        step_kernel,
        out_shape=(jax.ShapeDtypeStruct((SP, ROWS, 128), F32), jax.ShapeDtypeStruct((PX, PLANE), F32)),
        in_specs=[far] * 6,
        out_specs=(far, far),
        scratch_shapes=[
            plane, pltpu.VMEM((PLANE // 128, 8 * PX, 128), F32), plane, dma((2,)),
            pltpu.VMEM((SP, PX // SP, PLANE), F32), pltpu.VMEM((PX, PLANE), jnp.int32),
            pltpu.VMEM((FEATS, HID), BF16), pltpu.VMEM((HID,), F32), pltpu.VMEM((HID, BINS), BF16), pltpu.VMEM((BINS,), F32),
            dma((5,)), dma, dma((TEAM,)), dma((TEAM,)),
            pltpu.VMEM((HID, 128), F32), pltpu.VMEM((SP, ROWS, 128), F32), pltpu.VMEM((Y, ROWS, 128), F32),
            pltpu.VMEM((Z, ROWS, 128), F32), pltpu.VMEM((SP, ROWS, 128), F32), tile, tile, tile,
            dma((SP,)), dma((SP,)), dma((Y,)), dma((Y,)), dma((Z,)), dma((Z,)), dma((SP,)), dma((SP,)),
        ] + compute_scratch(),
        compiler_params=pltpu.CompilerParams(collective_id=0, has_side_effects=True, vmem_limit_bytes=56 * 2**20),
        name="train_step",
    )(frac, labels, cw, cb, ow, ob)


def close_kernel(grads_ref, loss_in, loss_ref, conv_ref, cbias_ref, out_ref, obias_ref, grads, sems):
    loss = pltpu.make_async_copy(loss_in, loss_ref, sems.at[0])
    load = pltpu.make_async_copy(grads_ref, grads, sems.at[1])
    load.start()
    loss.start()
    load.wait()
    full = jnp.concatenate([grads[i] for i in range(SP)], axis=0)
    conv_ref[...] = full[:FEATS, :HID]
    cbias_ref[...] = full[FEATS:FEATS + 1, :HID].reshape(HID)
    obias_ref[...] = full[FEATS + 1:FEATS + 2, :HID].reshape(BINS)
    out_ref[...] = full[:, HID:]
    loss.wait()


def close(grads, loss):
    vm, far = pl.BlockSpec(memory_space=pltpu.VMEM), pl.BlockSpec(memory_space=pl.ANY)
    return pl.pallas_call(
        close_kernel,
        out_shape=(jax.ShapeDtypeStruct((PX, PLANE), F32), jax.ShapeDtypeStruct((FEATS, HID), F32),
                   jax.ShapeDtypeStruct((HID,), F32), jax.ShapeDtypeStruct((HID, BINS), F32),
                   jax.ShapeDtypeStruct((BINS,), F32)),
        in_specs=[far, far],
        out_specs=(vm, vm, vm, vm, vm),
        scratch_shapes=[pltpu.VMEM((SP, ROWS, 128), F32), pltpu.SemaphoreType.DMA((2,))],
        compiler_params=pltpu.CompilerParams(vmem_limit_bytes=56 * 2**20),
        name="close_step",
    )(grads, loss)


def shards(fraction, labels, conv_weight, conv_bias, out_weight, out_bias):
    grads, loss = train_step(fraction.reshape(fraction.shape[1:]), labels.reshape(PX, PLANE),
                             conv_weight, conv_bias, out_weight, out_bias)
    loss, conv, cbias, out, obias = close(grads, loss)
    return loss.reshape(labels.shape), conv, cbias, out, obias


def solution(mesh):
    placed = (P("dp", None, "sp", "sec"), P("dp", ("sec", "sp"), None, None), P(), P(), P(), P())
    return jax.shard_map(
        shards,
        mesh=mesh,
        in_specs=placed,
        out_specs=(P("dp", ("sec", "sp"), None, None), P(), P(), P(), P()),
        check_vma=False,
    )
```

```python
import functools
import jax
import jax.numpy as jnp
from jax import lax
from jax.experimental import pallas as pl
from jax.experimental.pallas import tpu as pltpu
from jax.sharding import PartitionSpec as P

PX, PY, PZ = 32, 32, 32
PLANE = PY * PZ
HID = 64
BINS = 64
FEATS = 54
XB = 8
NB = PX // XB
GROUP = 24
KC = 9 * GROUP
KP = KC + 8
KO = HID + 16
TILE = 256
F32, BF16 = jnp.float32, jnp.bfloat16
LEAD = 2
CH = 2
HIDDEN_AT = (0, 6)
CONV_AT = (1, 3)
OUT_AT = (5, 7, 9, 11)
NT = (((1,), (1,)), ((), ()))
TN = (((0,), (0,)), ((), ()))


def iota(shape, axis):
    return lax.broadcasted_iota(jnp.int32, shape, axis)


def split3(value):
    high = value.astype(BF16)
    rest = value - high.astype(F32)
    mid = rest.astype(BF16)
    low = (rest - mid.astype(F32)).astype(BF16)
    return high.astype(F32), mid.astype(F32), low.astype(F32)


def column(row):
    n = row.shape[1]
    eye = iota((n, n), 0) == iota((n, n), 1)
    return jnp.sum(jnp.where(eye, row, 0.0), axis=1, keepdims=True)


def conv_rows(p_minus_x, shape, k_axis, c_axis):
    col = iota(shape, c_axis)
    k = iota(shape, k_axis)
    t = col // GROUP
    u = col - t * GROUP
    c = jnp.where(u >= 10, 1, 0)
    dx = u - 10 * c - p_minus_x
    return (col < KC) & (u < 20) & (dx >= 0) & (dx < 3) & (k == 18 * dx + 2 * t + c)


def prepare(cw_ref, cb_ref, ow_ref, ob_ref, wide_ref, owt_ref, owb_ref):
    cb = column(cb_ref[...].reshape(1, HID)) * 0.5
    ch, cm, cl = split3(cb)
    col = iota((HID, KP), 1)
    bias = jnp.where(col == KC, ch, jnp.where(col == KC + 1, cm, jnp.where(col == KC + 2, cl, 0.0)))
    cw = cw_ref[...]
    for x in range(XB):
        pick = jnp.where(conv_rows(x, (FEATS, KP), 0, 1), 0.5, 0.0).astype(BF16)
        row = lax.dot_general(cw, pick, TN, preferred_element_type=F32) + bias
        wide_ref[x * HID:(x + 1) * HID, :] = row.astype(BF16)
    ob = column(ob_ref[...].reshape(1, BINS))
    oh, om, ol = split3(ob)
    ow = ow_ref[...]
    eye = (iota((HID, KO), 0) == iota((HID, KO), 1)).astype(F32).astype(BF16)
    owt = lax.dot_general(ow, eye, TN, preferred_element_type=F32)
    col = iota((BINS, KO), 1)
    owt = owt + jnp.where(col == HID, oh, jnp.where(col == HID + 1, om, jnp.where(col == HID + 2, ol, 0.0)))
    owt_ref[...] = owt.astype(BF16)
    owb_ref[...] = (ow.astype(F32) * 0.5).astype(BF16)


def box(padded_ref, square, z_lo, z_hi, y_lo, y_hi):
    a, b, c = padded_ref[7:39, :], padded_ref[8:40, :], padded_ref[9:41, :]
    if square:
        s = a * a + b * b + c * c
    else:
        s = a + b + c
    s = s + jnp.where(z_lo, 0.0, pltpu.roll(s, 1, 1)) + jnp.where(z_hi, 0.0, pltpu.roll(s, PLANE - 1, 1))
    s = s + jnp.where(y_lo, 0.0, pltpu.roll(s, PZ, 1)) + jnp.where(y_hi, 0.0, pltpu.roll(s, PLANE - PZ, 1))
    return s / 27.0


def edges(shape):
    pos = iota(shape, 1)
    z = pos & (PZ - 1)
    return z == 0, z == PZ - 1, pos < PZ, pos >= PLANE - PZ


def filter_patch(patch_ref, pad_ref, f0_ref, f1_ref):
    for i in range(8):
        pad_ref[8 + 4 * i:12 + 4 * i, :] = patch_ref[i]
    z_lo, z_hi, y_lo, y_hi = edges((PX, PLANE))
    filt = box(pad_ref, False, z_lo, z_hi, y_lo, y_hi)
    f0_ref[8:40, :] = filt
    f1_ref[8:40, :] = box(pad_ref, True, z_lo, z_hi, y_lo, y_hi) - filt * filt


def stencil(f0_ref, f1_ref, join_ref, g_ref):
    z_lo, z_hi, y_lo, y_hi = edges((GROUP, PLANE))
    for b in range(NB):
        join_ref[0:10, :] = f0_ref[8 * b + 7:8 * b + 17, :]
        join_ref[10:20, :] = f1_ref[8 * b + 7:8 * b + 17, :]
        mid = join_ref[...]
        lo = jnp.where(z_lo, 0.0, pltpu.roll(mid, 1, 1))
        hi = jnp.where(z_hi, 0.0, pltpu.roll(mid, PLANE - 1, 1))
        parts = []
        for step_y in (-1, 0, 1):
            for v in (lo, mid, hi):
                if step_y == -1:
                    v = jnp.where(y_lo, 0.0, pltpu.roll(v, PZ, 1))
                elif step_y == 1:
                    v = jnp.where(y_hi, 0.0, pltpu.roll(v, PLANE - PZ, 1))
                parts.append(v)
        parts.append(jnp.ones((8, PLANE), F32))
        g_ref[b] = jnp.concatenate(parts, axis=0).astype(BF16)


def fold(v):
    return v[:, :128] + v[:, 128:]


def clear(bins_ref, d_ref, act_ref, low_ref, grad_ref, dconv_ref, dout_ref, hsum_ref, rsum_ref, pad_ref, f0_ref, f1_ref, join_ref):
    bins_ref[...] = iota((BINS, TILE), 0)
    for ref in (dconv_ref, dout_ref, hsum_ref, rsum_ref, grad_ref, d_ref.at[2], act_ref.at[2], low_ref.at[1]):
        ref[...] = jnp.zeros(ref.shape, ref.dtype)
    zero = jnp.zeros((8, PLANE), F32)
    for ref in (pad_ref, f0_ref, f1_ref):
        ref[0:8, :] = zero
        ref[40:48, :] = zero
    join_ref[20:24, :] = jnp.zeros((4, PLANE), F32)


def train(labels_ref, bins_ref, early_ref, wide_ref, owt_ref, owb_ref, g_ref, act_ref, d_ref, low_ref, grad_ref, z_ref, pick_ref, dconv_ref, dout_ref, hsum_ref, rsum_ref, scale):
    ones = jnp.ones((16, TILE), BF16)
    width = CH * TILE
    per = PLANE // width
    steps = NB * per
    tiles = [(c, x) for c in range(CH) for x in range(XB)]

    def span(c):
        return slice(c * TILE, (c + 1) * TILE)

    def place(step, c):
        return step // per, pl.ds(pl.multiple_of((step % per) * width + c * TILE, TILE), TILE)

    def within(step):
        return jnp.clip(step, 0, steps - 1)

    def hidden_dot(step, c):
        b, cols = place(within(step), c)
        return jnp.dot(wide_ref[...], g_ref[b, :, cols], preferred_element_type=F32)

    def silu(step, c, x, u_all):
        slot = lax.rem(step, 3)
        u = u_all[x * HID:(x + 1) * HID]
        t = jnp.tanh(u)
        w = 1.0 + t
        a = u * w
        act_ref[slot, x, :, span(c)] = a.astype(BF16)
        d_ref[slot, x, :, span(c)] = (w + a) - a * t

    def hidden(step):
        for c in range(CH):
            u_all = hidden_dot(step, c)
            for x in range(XB):
                silu(step, c, x, u_all)

    def logit(step, c, x):
        slot = lax.rem(step, 3)
        return jnp.dot(owt_ref[...], jnp.concatenate([act_ref[slot, x, :, span(c)], ones], axis=0), preferred_element_type=F32)

    def softmax(step, c, x, logits):
        b, cols = place(step, c)
        row = XB * b + x
        e = jnp.exp(logits)
        hot = jnp.where(bins_ref[...] == labels_ref[pl.ds(row, 1), cols], scale, 0.0)
        picked = logits * hot
        picked = sum(picked[8 * k:8 * k + 8] for k in range(BINS // 8))
        for half in range(TILE // 128):
            lane = (step % per) * (width // 128) + c * (TILE // 128) + half
            pick_ref[lane, pl.ds(pl.multiple_of(8 * row, 8), 8), :] = picked[:, 128 * half:128 * half + 128]
        total = jnp.sum(e, axis=0, keepdims=True)
        z_ref[pl.ds(row, 1), cols] = total
        r = e * (scale / total) - hot
        low_ref[lax.rem(step, 2), x, :, span(c)] = r.astype(BF16)
        return fold(r)

    def back(step, c, x):
        prod = jnp.dot(owb_ref[...], low_ref[lax.rem(step, 2), x, :, span(c)], preferred_element_type=F32)
        grad = prod * d_ref[lax.rem(step, 3), x, :, span(c)]
        grad_ref[lax.rem(step, 2), x * HID:(x + 1) * HID, span(c)] = grad.astype(BF16)
        return fold(grad)

    def out_grad(step, part, parts):
        xs = range(part * XB // parts, (part + 1) * XB // parts)
        dout_ref[...] += lax.dot_general(
            jnp.concatenate([act_ref[lax.rem(step, 3), x] for x in xs], axis=1),
            jnp.concatenate([low_ref[lax.rem(step, 2), x] for x in xs], axis=1), NT, preferred_element_type=F32)

    def conv_grad(step, at, part, parts):
        b = at // per
        cols = pl.ds(pl.multiple_of((at % per) * width, width), width)
        rows = slice(part * XB * HID // parts, (part + 1) * XB * HID // parts)
        dconv_ref[rows, :] += lax.dot_general(grad_ref[lax.rem(step, 2), rows, :], g_ref[b, :, cols], NT, preferred_element_type=F32)

    def add(total, term):
        return term if total is None else total + term

    hidden(0)
    for i in range(LEAD):
        early_ref[i] = logit(0, *tiles[i])

    def body(step, carry):
        old, oldest, ahead = step + 5, step + 4, step + 1
        hsum = rsum = None
        logits = {t: early_ref[i] for i, t in enumerate(tiles[:LEAD])}
        n = len(tiles)
        u_all = {}
        for i, t in enumerate(tiles):
            if i in HIDDEN_AT:
                u_all[HIDDEN_AT.index(i)] = hidden_dot(ahead, HIDDEN_AT.index(i))
            if i + LEAD < n:
                logits[tiles[i + LEAD]] = logit(step, *tiles[i + LEAD])
            if i in CONV_AT:
                conv_grad(oldest, within(step - 2), CONV_AT.index(i), len(CONV_AT))
            if i in OUT_AT:
                out_grad(old, OUT_AT.index(i), len(OUT_AT))
            hsum = add(hsum, back(old, *t))
            silu(ahead, *t, u_all[t[0]])
            rsum = add(rsum, softmax(step, *t, logits.pop(t)))
        for i in range(LEAD):
            early_ref[i] = logit(ahead, *tiles[i])
        rsum_ref[...] += rsum
        hsum_ref[...] += hsum
        return carry

    lax.fori_loop(0, steps, body, 0)
    hsum = None
    for t in tiles:
        hsum = add(hsum, back(steps - 1, *t))
    hsum_ref[...] += hsum
    conv_grad(steps - 2, steps - 2, 0, 1)
    out_grad(steps - 1, 0, 1)
    conv_grad(steps - 1, steps - 1, 0, 1)


def losses(z_ref, pick_ref, loss_ref, scale):
    for lane in range(PLANE // 128):
        cols = slice(128 * lane, 128 * lane + 128)
        picked = sum(pick_ref[lane, pl.ds(k, PX, stride=8), :] for k in range(8))
        loss_ref[:, cols] = jnp.log(z_ref[:, cols]) - picked / scale


def finish(dconv_ref, dout_ref, hsum_ref, rsum_ref, part_ref):
    total = dconv_ref[0:HID, :]
    for x in range(1, XB):
        total = total + pltpu.roll(dconv_ref[x * HID:(x + 1) * HID, :], KP - x, 1)
    col = iota((HID, KP), 1)
    hcol = jnp.sum(hsum_ref[...], axis=1, keepdims=True)
    rcol = jnp.sum(rsum_ref[...], axis=1, keepdims=True)
    total = jnp.where(col == KC, hcol, jnp.where(col == KC + 1, rcol, total))
    k, c = iota((HID, KP), 0), iota((HID, KP), 1)
    pick = conv_rows(0, (HID, KP), 0, 1) | ((k == FEATS) & (c == KC)) | ((k == FEATS + 1) & (c == KC + 1))
    rows = lax.dot_general(jnp.where(pick, 1.0, 0.0), total, NT, precision=lax.Precision.HIGHEST, preferred_element_type=F32)
    part_ref[:, 0:HID] = rows
    part_ref[:, HID:2 * HID] = dout_ref[...]


def compute_scratch():
    return [
        pltpu.VMEM((48, PLANE), F32), pltpu.VMEM((48, PLANE), F32), pltpu.VMEM((48, PLANE), F32),
        pltpu.VMEM((GROUP, PLANE), F32),
        pltpu.VMEM((NB, KP, PLANE), BF16),
        pltpu.VMEM((XB * HID, KP), BF16), pltpu.VMEM((BINS, KO), BF16), pltpu.VMEM((HID, BINS), BF16),
        pltpu.VMEM((3, XB, HID, CH * TILE), BF16), pltpu.VMEM((3, XB, HID, CH * TILE), F32),
        pltpu.VMEM((2, XB, BINS, CH * TILE), BF16), pltpu.VMEM((2, XB * HID, CH * TILE), BF16), pltpu.VMEM((BINS, TILE), jnp.int32), pltpu.VMEM((LEAD, BINS, TILE), F32),
        pltpu.VMEM((XB * HID, KP), F32), pltpu.VMEM((HID, BINS), F32),
        pltpu.VMEM((HID, 128), F32), pltpu.VMEM((BINS, 128), F32),
    ]


SEC, SP, YHI, Z = 4, 8, 2, 12
TEAM = SEC * SP
Y = SEC * YHI
ROWS = HID // SP
SCALE = 1.0 / 25165824
MESH = pl.DeviceIdType.MESH


def place_here():
    sec, sp, dp = lax.axis_index("sec"), lax.axis_index("sp"), lax.axis_index("dp")
    return sec, sp, dp // Z, lax.rem(dp, Z)


def flips(value):
    return value, value + 1 - 2 * lax.rem(value, 2), lax.rem(value + 2, 4), 3 - value


def sp_flips(sp):
    chips, core = flips(sp // 2), lax.rem(sp, 2)
    return [2 * chips[k // 2] + (1 - core if k % 2 else core) for k in range(SP)]


CHIP_HOPS = (0, 1, 2, 1)
SP_FAR = sorted(range(1, SP), key=lambda k: -CHIP_HOPS[k // 2])
TEAM_FAR = sorted(((a, k) for a in range(SEC) for k in range(SP) if a or k), key=lambda t: -t[0] - CHIP_HOPS[t[1] // 2])
Y_FAR = [(1, a) for a in (3, 2, 1, 0)] + [(0, a) for a in (3, 2, 1)]


def rings():
    sec, sp, yhi, z = place_here()
    secs, sps = flips(sec), sp_flips(sp)
    team = [(secs[a] * SP + sps[k], {"sec": secs[a], "sp": sps[k]}) for a, k in TEAM_FAR]
    row = [(sps[k], {"sp": sps[k]}) for k in SP_FAR]
    across = ((yhi, yhi * Z + z), (1 - yhi, (1 - yhi) * Z + z))
    ys = [(across[f][0] * SEC + secs[a], {"sec": secs[a], "dp": across[f][1]}) for f, a in Y_FAR]
    zs = []
    for i in sorted(range(1, Z), key=lambda i: -min(i, Z - i)):
        other = jnp.where(z + i >= Z, z + i - Z, z + i)
        zs.append((other, {"dp": yhi * Z + other}))
    return team, row, ys, zs


def greet(*groups):
    barrier = pltpu.get_barrier_semaphore()
    count = 0
    for group in groups:
        for _, device in group:
            pl.semaphore_signal(barrier, inc=1, device_id=device, device_id_type=MESH)
            count += 1
    pl.semaphore_wait(barrier, count)


def remote(src, dst, send_sem, recv_sem, device):
    return pltpu.make_async_remote_copy(
        src_ref=src, dst_ref=dst, send_sem=send_sem, recv_sem=recv_sem, device_id=device, device_id_type=MESH)


def relay(team, frac_ref, patch_ref, send_sem, recv_sem):
    sec, sp, _, _ = place_here()
    spot = patch_ref.at[sp, :, pl.ds(pl.multiple_of(sec * (PLANE // SEC), PLANE // SEC), PLANE // SEC)]
    for rank, device in team:
        remote(frac_ref.at[rank], spot, send_sem, recv_sem, device).start()
    pltpu.make_async_copy(frac_ref.at[sec * SP + sp], spot, recv_sem).start()

    def arrive():
        pltpu.make_async_copy(patch_ref, patch_ref, recv_sem).wait()

    def leave():
        sent = frac_ref.at[pl.ds(0, TEAM - 1)]
        remote(sent, sent, send_sem, recv_sem, team[0][1]).wait_send()

    return arrive, leave


def swap(ring, me, source, slots, send_sem, recv_sem, meanwhile=None):
    for rank, device in ring:
        remote(source(rank), slots.at[me], send_sem, recv_sem, device).start()
    if meanwhile is not None:
        meanwhile()
    others = slots.at[pl.ds(0, len(ring))]
    both = remote(others, others, send_sem, recv_sem, ring[0][1])
    both.wait_recv()
    return both.wait_send


def reduce_grads(meanwhile, row, ys, zs, part, first, second, third, result, piece, piece2, total, sends, recvs):
    sec, sp, yhi, z = place_here()

    def rows(rank):
        return part.at[pl.ds(pl.multiple_of(rank * ROWS, ROWS), ROWS), :]

    first[sp] = rows(sp)[...]
    leaves = [swap(row, sp, rows, first, sends.at[0], recvs.at[0])]
    piece[...] = jnp.sum(first[...], axis=0)
    y = yhi * SEC + sec
    second[y] = piece[...]
    leaves.append(swap(ys, y, lambda rank: piece, second, sends.at[1], recvs.at[1]))
    piece2[...] = jnp.sum(second[...], axis=0)
    third[z] = piece2[...]
    leaves.append(swap(zs, z, lambda rank: piece2, third, sends.at[2], recvs.at[2], meanwhile))
    total[...] = jnp.sum(third[...], axis=0)
    result[sp] = total[...]
    leaves.append(swap(row, sp, lambda rank: total, result, sends.at[3], recvs.at[3]))
    return leaves


def step_kernel(frac_ref, labels_ref, cw_ref, cb_ref, ow_ref, ob_ref, grads_ref, loss_ref,
                z, pick, loss, out_sems, patch, labels, cw, cb, ow, ob, in_sems, send_sems, recv_sems,
                part, first, second, third, result, piece, piece2, total,
                pad, f0, f1, join, g, wide, owt, owb, act, d, low, grad, bins, early, dconv, dout, hsum, rsum):
    loads = [pltpu.make_async_copy(src, dst, in_sems.at[i]) for i, (src, dst) in enumerate(
        ((cw_ref, cw), (cb_ref, cb), (ow_ref, ow), (ob_ref, ob), (labels_ref, labels)))]
    for load in loads:
        load.start()
    team, row, ys, zs = rings()
    greet(team, zs, ys[:SEC])
    arrive, leave = relay(team, frac_ref, patch, send_sems.at[4], recv_sems.at[4])
    for load in loads:
        load.wait()
    prepare(cw, cb, ow, ob, wide, owt, owb)
    clear(bins, d, act, low, grad, dconv, dout, hsum, rsum, pad, f0, f1, join)
    arrive()
    filter_patch(patch, pad, f0, f1)
    stencil(f0, f1, join, g)
    train(labels, bins, early, wide, owt, owb, g, act, d, low, grad, z, pick, dconv, dout, hsum, rsum, SCALE)
    finish(dconv, dout, hsum, rsum, part)

    def save_loss():
        losses(z, pick, loss, SCALE)
        pltpu.make_async_copy(loss, loss_ref, out_sems.at[0]).start()

    leaves = reduce_grads(save_loss, row, ys, zs, part, first, second, third, result, piece, piece2, total, send_sems, recv_sems)
    save = pltpu.make_async_copy(result, grads_ref, out_sems.at[1])
    save.start()
    for end in [leave] + leaves:
        end()
    pltpu.make_async_copy(loss, loss_ref, out_sems.at[0]).wait()
    save.wait()


def train_step(frac, labels, cw, cb, ow, ob):
    far = pl.BlockSpec(memory_space=pl.ANY)
    dma = pltpu.SemaphoreType.DMA
    tile = pltpu.VMEM((ROWS, 128), F32)
    plane = pltpu.VMEM((PX, PLANE), F32)
    return pl.pallas_call(
        step_kernel,
        out_shape=(jax.ShapeDtypeStruct((SP, ROWS, 128), F32), jax.ShapeDtypeStruct((PX, PLANE), F32)),
        in_specs=[far] * 6,
        out_specs=(far, far),
        scratch_shapes=[
            plane, pltpu.VMEM((PLANE // 128, 8 * PX, 128), F32), plane, dma((2,)),
            pltpu.VMEM((SP, PX // SP, PLANE), F32), pltpu.VMEM((PX, PLANE), jnp.int32),
            pltpu.VMEM((FEATS, HID), BF16), pltpu.VMEM((HID,), F32), pltpu.VMEM((HID, BINS), BF16), pltpu.VMEM((BINS,), F32),
            dma((5,)), dma((5,)), dma((5,)),
            pltpu.VMEM((HID, 128), F32), pltpu.VMEM((SP, ROWS, 128), F32), pltpu.VMEM((Y, ROWS, 128), F32),
            pltpu.VMEM((Z, ROWS, 128), F32), pltpu.VMEM((SP, ROWS, 128), F32), tile, tile, tile,
        ] + compute_scratch(),
        compiler_params=pltpu.CompilerParams(collective_id=0, has_side_effects=True, vmem_limit_bytes=56 * 2**20),
        name="train_step",
    )(frac, labels, cw, cb, ow, ob)


def close_kernel(grads_ref, loss_in, loss_ref, conv_ref, cbias_ref, out_ref, obias_ref, grads, sems):
    loss = pltpu.make_async_copy(loss_in, loss_ref, sems.at[0])
    load = pltpu.make_async_copy(grads_ref, grads, sems.at[1])
    load.start()
    loss.start()
    load.wait()
    full = jnp.concatenate([grads[i] for i in range(SP)], axis=0)
    conv_ref[...] = full[:FEATS, :HID]
    cbias_ref[...] = full[FEATS:FEATS + 1, :HID].reshape(HID)
    obias_ref[...] = full[FEATS + 1:FEATS + 2, :HID].reshape(BINS)
    out_ref[...] = full[:, HID:]
    loss.wait()


def close(grads, loss):
    vm, far = pl.BlockSpec(memory_space=pltpu.VMEM), pl.BlockSpec(memory_space=pl.ANY)
    return pl.pallas_call(
        close_kernel,
        out_shape=(jax.ShapeDtypeStruct((PX, PLANE), F32), jax.ShapeDtypeStruct((FEATS, HID), F32),
                   jax.ShapeDtypeStruct((HID,), F32), jax.ShapeDtypeStruct((HID, BINS), F32),
                   jax.ShapeDtypeStruct((BINS,), F32)),
        in_specs=[far, far],
        out_specs=(vm, vm, vm, vm, vm),
        scratch_shapes=[pltpu.VMEM((SP, ROWS, 128), F32), pltpu.SemaphoreType.DMA((2,))],
        compiler_params=pltpu.CompilerParams(vmem_limit_bytes=56 * 2**20),
        name="close_step",
    )(grads, loss)


def shards(fraction, labels, conv_weight, conv_bias, out_weight, out_bias):
    grads, loss = train_step(fraction.reshape(fraction.shape[1:]), labels.reshape(PX, PLANE),
                             conv_weight, conv_bias, out_weight, out_bias)
    loss, conv, cbias, out, obias = close(grads, loss)
    return loss.reshape(labels.shape), conv, cbias, out, obias


def solution(mesh):
    placed = (P("dp", None, "sp", "sec"), P("dp", ("sec", "sp"), None, None), P(), P(), P(), P())
    return jax.shard_map(
        shards,
        mesh=mesh,
        in_specs=placed,
        out_specs=(P("dp", ("sec", "sp"), None, None), P(), P(), P(), P()),
        check_vma=False,
    )
```

```python
import functools
import jax
import jax.numpy as jnp
from jax import lax
from jax.experimental import pallas as pl
from jax.experimental.pallas import tpu as pltpu
from jax.sharding import PartitionSpec as P

PX, PY, PZ = 32, 32, 32
PLANE = PY * PZ
HID = 64
BINS = 64
FEATS = 54
XB = 8
NB = PX // XB
GROUP = 24
KC = 9 * GROUP
KP = KC + 8
KO = HID + 16
TILE = 256
F32, BF16 = jnp.float32, jnp.bfloat16
LEAD = 2
CH = 2
HIDDEN_AT = (0, 4)
CONV_AT = (1, 3)
OUT_AT = (5, 7, 9, 11)
NT = (((1,), (1,)), ((), ()))
TN = (((0,), (0,)), ((), ()))


def iota(shape, axis):
    return lax.broadcasted_iota(jnp.int32, shape, axis)


def split3(value):
    high = value.astype(BF16)
    rest = value - high.astype(F32)
    mid = rest.astype(BF16)
    low = (rest - mid.astype(F32)).astype(BF16)
    return high.astype(F32), mid.astype(F32), low.astype(F32)


def column(row):
    n = row.shape[1]
    eye = iota((n, n), 0) == iota((n, n), 1)
    return jnp.sum(jnp.where(eye, row, 0.0), axis=1, keepdims=True)


def conv_rows(p_minus_x, shape, k_axis, c_axis):
    col = iota(shape, c_axis)
    k = iota(shape, k_axis)
    t = col // GROUP
    u = col - t * GROUP
    c = jnp.where(u >= 10, 1, 0)
    dx = u - 10 * c - p_minus_x
    return (col < KC) & (u < 20) & (dx >= 0) & (dx < 3) & (k == 18 * dx + 2 * t + c)


def prepare(cw_ref, cb_ref, ow_ref, ob_ref, wide_ref, owt_ref, owb_ref):
    cb = column(cb_ref[...].reshape(1, HID)) * 0.5
    ch, cm, cl = split3(cb)
    col = iota((HID, KP), 1)
    bias = jnp.where(col == KC, ch, jnp.where(col == KC + 1, cm, jnp.where(col == KC + 2, cl, 0.0)))
    cw = cw_ref[...]
    for x in range(XB):
        pick = jnp.where(conv_rows(x, (FEATS, KP), 0, 1), 0.5, 0.0).astype(BF16)
        row = lax.dot_general(cw, pick, TN, preferred_element_type=F32) + bias
        wide_ref[x * HID:(x + 1) * HID, :] = row.astype(BF16)
    ob = column(ob_ref[...].reshape(1, BINS))
    oh, om, ol = split3(ob)
    ow = ow_ref[...]
    eye = (iota((HID, KO), 0) == iota((HID, KO), 1)).astype(F32).astype(BF16)
    owt = lax.dot_general(ow, eye, TN, preferred_element_type=F32)
    col = iota((BINS, KO), 1)
    owt = owt + jnp.where(col == HID, oh, jnp.where(col == HID + 1, om, jnp.where(col == HID + 2, ol, 0.0)))
    owt_ref[...] = owt.astype(BF16)
    owb_ref[...] = (ow.astype(F32) * 0.5).astype(BF16)


def shift_z(parts, step):
    z = iota(parts[0].shape, 1) & (PZ - 1)
    edge = z == (0 if step > 0 else PZ - 1)
    return [jnp.where(edge, 0.0, pltpu.roll(part, step % 128, 1)) for part in parts]


def rows_wrap(step):
    lane = iota((8, 128), 1)
    return lane < PZ if step > 0 else lane >= 128 - PZ


def shift_y(parts, step):
    wraps = jnp.broadcast_to(rows_wrap(step)[0:1], parts[0].shape)
    rolled = [pltpu.roll(part, step * PZ % 128, 1) for part in parts]
    ends = [jnp.zeros_like(parts[0])]
    near = ends + rolled[:-1] if step > 0 else rolled[1:] + ends
    return [jnp.where(wraps, other, own) for other, own in zip(near, rolled)]


def box(planes):
    none = [jnp.zeros_like(planes[0])]
    s = [a + b + c for a, b, c in zip(none + planes[:-1], planes, planes[1:] + none)]
    s = [mid + lo + hi for mid, lo, hi in zip(s, shift_z(s, 1), shift_z(s, -1))]
    group = iota((8, 128), 0)
    sums = []
    for v in s:
        for step, last in ((1, 0), (-1, 7)):
            rolled = pltpu.roll(v, step * PZ % 128, 1)
            near = jnp.where(group == last, 0.0, pltpu.roll(rolled, step % 8, 0))
            sums.append(jnp.where(rows_wrap(step), near, rolled))
    return [(v + sums[2 * k] + sums[2 * k + 1]) / 27.0 for k, v in enumerate(s)]


def filter_patch(patch_ref, f0_ref, f1_ref):
    planes = [patch_ref[p // 4, pl.ds(p % 4, 8, stride=4), :] for p in range(PX)]
    filt = box(planes)
    square = box([p * p for p in planes])
    for p in range(PX):
        rows = slice(8 * p + 8, 8 * p + 16)
        f0_ref[rows, :] = filt[p]
        f1_ref[rows, :] = square[p] - filt[p] * filt[p]


def stencil(f0_ref, f1_ref, join_ref, g_ref):
    ones = jnp.ones((8, 128), F32)
    for b in range(NB):
        mid = []
        for k in range(PLANE // 128):
            cols = slice(128 * k, 128 * k + 128)
            join_ref[0:10, cols] = f0_ref[pl.ds(64 * b + k, 10, stride=8), :]
            join_ref[10:20, cols] = f1_ref[pl.ds(64 * b + k, 10, stride=8), :]
            mid.append(join_ref[:, cols])
        taps = []
        for step_y in (1, 0, -1):
            row = shift_y(mid, step_y) if step_y else mid
            taps += [shift_z(row, 1), row, shift_z(row, -1)]
        for k in range(PLANE // 128):
            rows = jnp.concatenate([tap[k] for tap in taps] + [ones], axis=0)
            g_ref[b, :, 128 * k:128 * k + 128] = rows.astype(BF16)


def fold(v):
    return v[:, :128] + v[:, 128:]


def clear(bins_ref, d_ref, act_ref, low_ref, grad_ref, dconv_ref, dout_ref, hsum_ref, rsum_ref, f0_ref, f1_ref, join_ref):
    bins_ref[...] = iota((BINS, TILE), 0)
    for ref in (dconv_ref, dout_ref, hsum_ref, rsum_ref, grad_ref, d_ref.at[2], act_ref.at[2], low_ref.at[1]):
        ref[...] = jnp.zeros(ref.shape, ref.dtype)
    zero = jnp.zeros((8, 128), F32)
    for ref in (f0_ref, f1_ref):
        ref[0:8, :] = zero
        ref[8 * PX + 8:8 * PX + 16, :] = zero
    join_ref[20:24, :] = jnp.zeros((4, PLANE), F32)


def train(labels_ref, bins_ref, early_ref, wide_ref, owt_ref, owb_ref, g_ref, act_ref, d_ref, low_ref, grad_ref, z_ref, pick_ref, dconv_ref, dout_ref, hsum_ref, rsum_ref, scale):
    ones = jnp.ones((16, TILE), BF16)
    width = CH * TILE
    per = PLANE // width
    steps = NB * per
    tiles = [(c, x) for c in range(CH) for x in range(XB)]

    def span(c):
        return slice(c * TILE, (c + 1) * TILE)

    def place(step, c):
        return step // per, pl.ds(pl.multiple_of((step % per) * width + c * TILE, TILE), TILE)

    def within(step):
        return jnp.clip(step, 0, steps - 1)

    def hidden_dot(step, c):
        b, cols = place(within(step), c)
        return jnp.dot(wide_ref[...], g_ref[b, :, cols], preferred_element_type=F32)

    def silu(step, c, x, u_all):
        slot = lax.rem(step, 3)
        u = u_all[x * HID:(x + 1) * HID]
        t = jnp.tanh(u)
        w = 1.0 + t
        a = u * w
        act_ref[slot, x, :, span(c)] = a.astype(BF16)
        d_ref[slot, x, :, span(c)] = (w + a) - a * t

    def hidden(step):
        for c in range(CH):
            u_all = hidden_dot(step, c)
            for x in range(XB):
                silu(step, c, x, u_all)

    def logit(step, c, x):
        slot = lax.rem(step, 3)
        return jnp.dot(owt_ref[...], jnp.concatenate([act_ref[slot, x, :, span(c)], ones], axis=0), preferred_element_type=F32)

    def softmax(step, c, x, logits):
        b, cols = place(step, c)
        row = XB * b + x
        e = jnp.exp(logits)
        hot = jnp.where(bins_ref[...] == labels_ref[pl.ds(row, 1), cols], scale, 0.0)
        picked = logits * hot
        picked = sum(picked[8 * k:8 * k + 8] for k in range(BINS // 8))
        for half in range(TILE // 128):
            lane = (step % per) * (width // 128) + c * (TILE // 128) + half
            pick_ref[lane, pl.ds(pl.multiple_of(8 * row, 8), 8), :] = picked[:, 128 * half:128 * half + 128]
        total = jnp.sum(e, axis=0, keepdims=True)
        z_ref[pl.ds(row, 1), cols] = total
        r = e * (scale / total) - hot
        low_ref[lax.rem(step, 2), x, :, span(c)] = r.astype(BF16)
        return fold(r)

    def back(step, c, x):
        prod = jnp.dot(owb_ref[...], low_ref[lax.rem(step, 2), x, :, span(c)], preferred_element_type=F32)
        grad = prod * d_ref[lax.rem(step, 3), x, :, span(c)]
        grad_ref[lax.rem(step, 2), x * HID:(x + 1) * HID, span(c)] = grad.astype(BF16)
        return fold(grad)

    def out_grad(step, part, parts):
        xs = range(part * XB // parts, (part + 1) * XB // parts)
        dout_ref[...] += lax.dot_general(
            jnp.concatenate([act_ref[lax.rem(step, 3), x] for x in xs], axis=1),
            jnp.concatenate([low_ref[lax.rem(step, 2), x] for x in xs], axis=1), NT, preferred_element_type=F32)

    def conv_grad(step, at, part, parts):
        b = at // per
        cols = pl.ds(pl.multiple_of((at % per) * width, width), width)
        rows = slice(part * XB * HID // parts, (part + 1) * XB * HID // parts)
        dconv_ref[rows, :] += lax.dot_general(grad_ref[lax.rem(step, 2), rows, :], g_ref[b, :, cols], NT, preferred_element_type=F32)

    def add(total, term):
        return term if total is None else total + term

    hidden(0)
    for i in range(LEAD):
        early_ref[i] = logit(0, *tiles[i])

    def body(step, carry):
        old, oldest, ahead = step + 5, step + 4, step + 1
        hsum = rsum = None
        logits = {t: early_ref[i] for i, t in enumerate(tiles[:LEAD])}
        n = len(tiles)
        u_all = {}
        for i, t in enumerate(tiles):
            if i in HIDDEN_AT:
                u_all[HIDDEN_AT.index(i)] = hidden_dot(ahead, HIDDEN_AT.index(i))
            hsum = add(hsum, back(old, *t))
            if i in CONV_AT:
                conv_grad(oldest, within(step - 2), CONV_AT.index(i), len(CONV_AT))
            if i in OUT_AT:
                out_grad(old, OUT_AT.index(i), len(OUT_AT))
            if i + LEAD < n:
                logits[tiles[i + LEAD]] = logit(step, *tiles[i + LEAD])
            silu(ahead, *t, u_all[t[0]])
            rsum = add(rsum, softmax(step, *t, logits.pop(t)))
        for i in range(LEAD):
            early_ref[i] = logit(ahead, *tiles[i])
        rsum_ref[...] += rsum
        hsum_ref[...] += hsum
        return carry

    lax.fori_loop(0, steps, body, 0)
    hsum = None
    for t in tiles:
        hsum = add(hsum, back(steps - 1, *t))
    hsum_ref[...] += hsum
    for k in range(2):
        conv_grad(steps - 1, steps - 1, k, 2)
        conv_grad(steps - 2, steps - 2, k, 2)
    out_grad(steps - 1, 0, 1)


def losses(z_ref, pick_ref, loss_ref, scale):
    for lane in range(PLANE // 128):
        cols = slice(128 * lane, 128 * lane + 128)
        picked = sum(pick_ref[lane, pl.ds(k, PX, stride=8), :] for k in range(8))
        loss_ref[:, cols] = jnp.log(z_ref[:, cols]) - picked / scale


def finish(dconv_ref, dout_ref, hsum_ref, rsum_ref, part_ref):
    total = dconv_ref[0:HID, :]
    for x in range(1, XB):
        total = total + pltpu.roll(dconv_ref[x * HID:(x + 1) * HID, :], KP - x, 1)
    col = iota((HID, KP), 1)
    hcol = jnp.sum(hsum_ref[...], axis=1, keepdims=True)
    rcol = jnp.sum(rsum_ref[...], axis=1, keepdims=True)
    total = jnp.where(col == KC, hcol, jnp.where(col == KC + 1, rcol, total))
    k, c = iota((HID, KP), 0), iota((HID, KP), 1)
    pick = conv_rows(0, (HID, KP), 0, 1) | ((k == FEATS) & (c == KC)) | ((k == FEATS + 1) & (c == KC + 1))
    rows = lax.dot_general(jnp.where(pick, 1.0, 0.0), total, NT, precision=lax.Precision.HIGHEST, preferred_element_type=F32)
    part_ref[:, 0:HID] = rows
    part_ref[:, HID:2 * HID] = dout_ref[...]


def compute_scratch():
    return [
        pltpu.VMEM((8 * PX + 16, 128), F32), pltpu.VMEM((8 * PX + 16, 128), F32),
        pltpu.VMEM((GROUP, PLANE), F32),
        pltpu.VMEM((NB, KP, PLANE), BF16),
        pltpu.VMEM((XB * HID, KP), BF16), pltpu.VMEM((BINS, KO), BF16), pltpu.VMEM((HID, BINS), BF16),
        pltpu.VMEM((3, XB, HID, CH * TILE), BF16), pltpu.VMEM((3, XB, HID, CH * TILE), F32),
        pltpu.VMEM((2, XB, BINS, CH * TILE), BF16), pltpu.VMEM((2, XB * HID, CH * TILE), BF16), pltpu.VMEM((BINS, TILE), jnp.int32), pltpu.VMEM((LEAD, BINS, TILE), F32),
        pltpu.VMEM((XB * HID, KP), F32), pltpu.VMEM((HID, BINS), F32),
        pltpu.VMEM((HID, 128), F32), pltpu.VMEM((BINS, 128), F32),
    ]


SEC, SP, YHI, Z = 4, 8, 2, 12
TEAM = SEC * SP
Y = SEC * YHI
ROWS = HID // SP
SCALE = 1.0 / 25165824
MESH = pl.DeviceIdType.MESH


def place_here():
    sec, sp, dp = lax.axis_index("sec"), lax.axis_index("sp"), lax.axis_index("dp")
    return sec, sp, dp // Z, lax.rem(dp, Z)


def flips(value):
    return value, value + 1 - 2 * lax.rem(value, 2), lax.rem(value + 2, 4), 3 - value


def sp_flips(sp):
    chips, core = flips(sp // 2), lax.rem(sp, 2)
    return [2 * chips[k // 2] + (1 - core if k % 2 else core) for k in range(SP)]


CHIP_HOPS = (0, 1, 2, 1)
SP_FAR = sorted(range(1, SP), key=lambda k: -CHIP_HOPS[k // 2])
TEAM_FAR = sorted(((a, k) for a in range(SEC) for k in range(SP) if a or k), key=lambda t: -t[0] - CHIP_HOPS[t[1] // 2])
Y_FAR = [(1, a) for a in (3, 2, 1, 0)] + [(0, a) for a in (3, 2, 1)]


def rings():
    sec, sp, yhi, z = place_here()
    secs, sps = flips(sec), sp_flips(sp)
    team = [(secs[a] * SP + sps[k], {"sec": secs[a], "sp": sps[k]}) for a, k in TEAM_FAR]
    row = [(sps[k], {"sp": sps[k]}) for k in SP_FAR]
    across = ((yhi, yhi * Z + z), (1 - yhi, (1 - yhi) * Z + z))
    ys = [(across[f][0] * SEC + secs[a], {"sec": secs[a], "dp": across[f][1]}) for f, a in Y_FAR]
    zs = []
    for i in sorted(range(1, Z), key=lambda i: -min(i, Z - i)):
        other = jnp.where(z + i >= Z, z + i - Z, z + i)
        zs.append((other, {"dp": yhi * Z + other}))
    return team, row, ys, zs


def greet(*groups):
    barrier = pltpu.get_barrier_semaphore()
    count = 0
    for group in groups:
        for _, device in group:
            pl.semaphore_signal(barrier, inc=1, device_id=device, device_id_type=MESH)
            count += 1
    pl.semaphore_wait(barrier, count)


def remote(src, dst, send_sem, recv_sem, device):
    return pltpu.make_async_remote_copy(
        src_ref=src, dst_ref=dst, send_sem=send_sem, recv_sem=recv_sem, device_id=device, device_id_type=MESH)


def relay(team, frac_ref, patch_ref, send_sem, recv_sem):
    sec, sp, _, _ = place_here()
    spot = patch_ref.at[sp, pl.ds(pl.multiple_of(8 * sec, 8), 8), :]
    for rank, device in team:
        remote(frac_ref.at[rank], spot, send_sem, recv_sem, device).start()
    pltpu.make_async_copy(frac_ref.at[sec * SP + sp], spot, recv_sem).start()

    def arrive():
        pltpu.make_async_copy(patch_ref, patch_ref, recv_sem).wait()

    def leave():
        sent = frac_ref.at[pl.ds(0, TEAM - 1)]
        remote(sent, sent, send_sem, recv_sem, team[0][1]).wait_send()

    return arrive, leave


def swap(ring, me, source, slots, send_sem, recv_sem, meanwhile=None):
    for rank, device in ring:
        remote(source(rank), slots.at[me], send_sem, recv_sem, device).start()
    if meanwhile is not None:
        meanwhile()
    others = slots.at[pl.ds(0, len(ring))]
    both = remote(others, others, send_sem, recv_sem, ring[0][1])
    both.wait_recv()
    return both.wait_send


def reduce_grads(meanwhile, row, ys, zs, part, first, second, third, result_ref, piece, piece2, total, sends, recvs):
    sec, sp, yhi, z = place_here()

    def rows(rank):
        return part.at[pl.ds(pl.multiple_of(rank * ROWS, ROWS), ROWS), :]

    first[sp] = rows(sp)[...]
    leaves = [swap(row, sp, rows, first, sends.at[0], recvs.at[0])]
    piece[...] = jnp.sum(first[...], axis=0)
    y = yhi * SEC + sec
    second[y] = piece[...]
    leaves.append(swap(ys, y, lambda rank: piece, second, sends.at[1], recvs.at[1]))
    piece2[...] = jnp.sum(second[...], axis=0)
    third[z] = piece2[...]
    leaves.append(swap(zs, z, lambda rank: piece2, third, sends.at[2], recvs.at[2], meanwhile))
    total[...] = jnp.sum(third[...], axis=0)
    mine = pltpu.make_async_copy(total, result_ref.at[sp], sends.at[5])
    mine.start()
    leaves.append(swap(row, sp, lambda rank: total, result_ref, sends.at[3], recvs.at[3]))
    return leaves + [mine.wait]


def step_kernel(frac_ref, labels_ref, cw_ref, cb_ref, ow_ref, ob_ref, grads_ref, loss_ref,
                z, pick, loss, out_sem, patch, labels, cw, cb, ow, ob, in_sems, send_sems, recv_sems,
                part, first, second, third, piece, piece2, total,
                f0, f1, join, g, wide, owt, owb, act, d, low, grad, bins, early, dconv, dout, hsum, rsum):
    loads = [pltpu.make_async_copy(src, dst, in_sems.at[i]) for i, (src, dst) in enumerate(
        ((cw_ref, cw), (cb_ref, cb), (ow_ref, ow), (ob_ref, ob), (labels_ref, labels)))]
    for load in loads:
        load.start()
    team, row, ys, zs = rings()
    greet(team, zs, ys[:SEC])
    arrive, leave = relay(team, frac_ref, patch, send_sems.at[4], recv_sems.at[4])
    for load in loads:
        load.wait()
    prepare(cw, cb, ow, ob, wide, owt, owb)
    clear(bins, d, act, low, grad, dconv, dout, hsum, rsum, f0, f1, join)
    arrive()
    filter_patch(patch, f0, f1)
    stencil(f0, f1, join, g)
    train(labels, bins, early, wide, owt, owb, g, act, d, low, grad, z, pick, dconv, dout, hsum, rsum, SCALE)
    finish(dconv, dout, hsum, rsum, part)

    def save_loss():
        losses(z, pick, loss, SCALE)
        pltpu.make_async_copy(loss, loss_ref, out_sem).start()

    leaves = reduce_grads(save_loss, row, ys, zs, part, first, second, third, grads_ref, piece, piece2, total, send_sems, recv_sems)
    for end in [leave] + leaves:
        end()
    pltpu.make_async_copy(loss, loss_ref, out_sem).wait()


def train_step(frac, labels, cw, cb, ow, ob):
    far = pl.BlockSpec(memory_space=pl.ANY)
    dma = pltpu.SemaphoreType.DMA
    tile = pltpu.VMEM((ROWS, 128), F32)
    plane = pltpu.VMEM((PX, PLANE), F32)
    return pl.pallas_call(
        step_kernel,
        out_shape=(jax.ShapeDtypeStruct((SP, ROWS, 128), F32), jax.ShapeDtypeStruct((PX, PLANE), F32)),
        in_specs=[far] * 6,
        out_specs=(far, far),
        scratch_shapes=[
            plane, pltpu.VMEM((PLANE // 128, 8 * PX, 128), F32), plane, dma,
            pltpu.VMEM((SP, 8 * SEC, 128), F32), pltpu.VMEM((PX, PLANE), jnp.int32),
            pltpu.VMEM((FEATS, HID), BF16), pltpu.VMEM((HID,), F32), pltpu.VMEM((HID, BINS), BF16), pltpu.VMEM((BINS,), F32),
            dma((5,)), dma((6,)), dma((5,)),
            pltpu.VMEM((HID, 128), F32), pltpu.VMEM((SP, ROWS, 128), F32), pltpu.VMEM((Y, ROWS, 128), F32),
            pltpu.VMEM((Z, ROWS, 128), F32), tile, tile, tile,
        ] + compute_scratch(),
        compiler_params=pltpu.CompilerParams(collective_id=0, has_side_effects=True, vmem_limit_bytes=56 * 2**20),
        name="train_step",
    )(frac, labels, cw, cb, ow, ob)


def close_kernel(grads_ref, loss_in, loss_ref, conv_ref, cbias_ref, out_ref, obias_ref, grads, sems):
    loss = pltpu.make_async_copy(loss_in, loss_ref, sems.at[0])
    load = pltpu.make_async_copy(grads_ref, grads, sems.at[1])
    load.start()
    loss.start()
    load.wait()
    full = jnp.concatenate([grads[i] for i in range(SP)], axis=0)
    conv_ref[...] = full[:FEATS, :HID]
    cbias_ref[...] = full[FEATS:FEATS + 1, :HID].reshape(HID)
    obias_ref[...] = full[FEATS + 1:FEATS + 2, :HID].reshape(BINS)
    out_ref[...] = full[:, HID:]
    loss.wait()


def close(grads, loss):
    vm, far = pl.BlockSpec(memory_space=pltpu.VMEM), pl.BlockSpec(memory_space=pl.ANY)
    return pl.pallas_call(
        close_kernel,
        out_shape=(jax.ShapeDtypeStruct((PX, PLANE), F32), jax.ShapeDtypeStruct((FEATS, HID), F32),
                   jax.ShapeDtypeStruct((HID,), F32), jax.ShapeDtypeStruct((HID, BINS), F32),
                   jax.ShapeDtypeStruct((BINS,), F32)),
        in_specs=[far, far],
        out_specs=(vm, vm, vm, vm, vm),
        scratch_shapes=[pltpu.VMEM((SP, ROWS, 128), F32), pltpu.SemaphoreType.DMA((2,))],
        compiler_params=pltpu.CompilerParams(vmem_limit_bytes=56 * 2**20),
        name="close_step",
    )(grads, loss)


def shards(fraction, labels, conv_weight, conv_bias, out_weight, out_bias):
    blocks = fraction.reshape(TEAM, 4, 2, 128).transpose(0, 2, 1, 3).reshape(TEAM, 8, 128)
    grads, loss = train_step(blocks, labels.reshape(PX, PLANE),
                             conv_weight, conv_bias, out_weight, out_bias)
    loss, conv, cbias, out, obias = close(grads, loss)
    return loss.reshape(labels.shape), conv, cbias, out, obias


def solution(mesh):
    placed = (P("dp", None, "sp", "sec"), P("dp", ("sec", "sp"), None, None), P(), P(), P(), P())
    return jax.shard_map(
        shards,
        mesh=mesh,
        in_specs=placed,
        out_specs=(P("dp", ("sec", "sp"), None, None), P(), P(), P(), P()),
        check_vma=False,
    )
```

```python
import functools
import jax
import jax.numpy as jnp
from jax import lax
from jax.experimental import pallas as pl
from jax.experimental.pallas import tpu as pltpu
from jax.sharding import PartitionSpec as P

PX, PY, PZ = 32, 32, 32
PLANE = PY * PZ
HID = 64
BINS = 64
FEATS = 54
XB = 8
NB = PX // XB
GROUP = 24
KC = 9 * GROUP
KP = KC + 8
KO = HID + 16
TILE = 256
F32, BF16 = jnp.float32, jnp.bfloat16
LEAD = 2
CH = 2
HIDDEN_AT = (0, 4)
CONV_AT = (1, 3)
OUT_AT = (5, 7, 9, 11)
NT = (((1,), (1,)), ((), ()))
TN = (((0,), (0,)), ((), ()))


def iota(shape, axis):
    return lax.broadcasted_iota(jnp.int32, shape, axis)


def split3(value):
    high = value.astype(BF16)
    rest = value - high.astype(F32)
    mid = rest.astype(BF16)
    low = (rest - mid.astype(F32)).astype(BF16)
    return high.astype(F32), mid.astype(F32), low.astype(F32)


def column(row):
    n = row.shape[1]
    eye = iota((n, n), 0) == iota((n, n), 1)
    return jnp.sum(jnp.where(eye, row, 0.0), axis=1, keepdims=True)


def conv_rows(p_minus_x, shape, k_axis, c_axis):
    col = iota(shape, c_axis)
    k = iota(shape, k_axis)
    t = col // GROUP
    u = col - t * GROUP
    c = jnp.where(u >= 10, 1, 0)
    dx = u - 10 * c - p_minus_x
    return (col < KC) & (u < 20) & (dx >= 0) & (dx < 3) & (k == 18 * dx + 2 * t + c)


def prepare(cw_ref, cb_ref, ow_ref, ob_ref, wide_ref, owt_ref, owb_ref):
    cb = column(cb_ref[...].reshape(1, HID)) * 0.5
    ch, cm, cl = split3(cb)
    col = iota((HID, KP), 1)
    bias = jnp.where(col == KC, ch, jnp.where(col == KC + 1, cm, jnp.where(col == KC + 2, cl, 0.0)))
    cw = cw_ref[...]
    for x in range(XB):
        pick = jnp.where(conv_rows(x, (FEATS, KP), 0, 1), 0.5, 0.0).astype(BF16)
        row = lax.dot_general(cw, pick, TN, preferred_element_type=F32) + bias
        wide_ref[x * HID:(x + 1) * HID, :] = row.astype(BF16)
    ob = column(ob_ref[...].reshape(1, BINS))
    oh, om, ol = split3(ob)
    ow = ow_ref[...]
    eye = (iota((HID, KO), 0) == iota((HID, KO), 1)).astype(F32).astype(BF16)
    owt = lax.dot_general(ow, eye, TN, preferred_element_type=F32)
    col = iota((BINS, KO), 1)
    owt = owt + jnp.where(col == HID, oh, jnp.where(col == HID + 1, om, jnp.where(col == HID + 2, ol, 0.0)))
    owt_ref[...] = owt.astype(BF16)
    owb_ref[...] = (ow.astype(F32) * 0.5).astype(BF16)


def shift_z(parts, step):
    z = iota(parts[0].shape, 1) & (PZ - 1)
    edge = z == (0 if step > 0 else PZ - 1)
    return [jnp.where(edge, 0.0, pltpu.roll(part, step % 128, 1)) for part in parts]


def rows_wrap(step):
    lane = iota((8, 128), 1)
    return lane < PZ if step > 0 else lane >= 128 - PZ


def shift_y(parts, step):
    wraps = jnp.broadcast_to(rows_wrap(step)[0:1], parts[0].shape)
    rolled = [pltpu.roll(part, step * PZ % 128, 1) for part in parts]
    ends = [jnp.zeros_like(parts[0])]
    near = ends + rolled[:-1] if step > 0 else rolled[1:] + ends
    return [jnp.where(wraps, other, own) for other, own in zip(near, rolled)]


def box(planes):
    none = [jnp.zeros_like(planes[0])]
    s = [a + b + c for a, b, c in zip(none + planes[:-1], planes, planes[1:] + none)]
    s = [mid + lo + hi for mid, lo, hi in zip(s, shift_z(s, 1), shift_z(s, -1))]
    group = iota((8, 128), 0)
    sums = []
    for v in s:
        for step, last in ((1, 0), (-1, 7)):
            rolled = pltpu.roll(v, step * PZ % 128, 1)
            near = jnp.where(group == last, 0.0, pltpu.roll(rolled, step % 8, 0))
            sums.append(jnp.where(rows_wrap(step), near, rolled))
    return [(v + sums[2 * k] + sums[2 * k + 1]) / 27.0 for k, v in enumerate(s)]


def filter_patch(patch_ref, f0_ref, f1_ref):
    planes = [patch_ref[p // 4, pl.ds(p % 4, 8, stride=4), :] for p in range(PX)]
    filt = box(planes)
    square = box([p * p for p in planes])
    for p in range(PX):
        rows = slice(8 * p + 8, 8 * p + 16)
        f0_ref[rows, :] = filt[p]
        f1_ref[rows, :] = square[p] - filt[p] * filt[p]


def stencil(f0_ref, f1_ref, join_ref, g_ref):
    ones = jnp.ones((8, 128), F32)
    for b in range(NB):
        mid = []
        for k in range(PLANE // 128):
            cols = slice(128 * k, 128 * k + 128)
            join_ref[0:10, cols] = f0_ref[pl.ds(64 * b + k, 10, stride=8), :]
            join_ref[10:20, cols] = f1_ref[pl.ds(64 * b + k, 10, stride=8), :]
            mid.append(join_ref[:, cols])
        taps = []
        for step_y in (1, 0, -1):
            row = shift_y(mid, step_y) if step_y else mid
            taps += [shift_z(row, 1), row, shift_z(row, -1)]
        for k in range(PLANE // 128):
            rows = jnp.concatenate([tap[k] for tap in taps] + [ones], axis=0)
            g_ref[b, :, 128 * k:128 * k + 128] = rows.astype(BF16)


def fold(v):
    return v[:, :128] + v[:, 128:]


def clear(d_ref, act_ref, low_ref, grad_ref, dconv_ref, dout_ref, hsum_ref, rsum_ref, f0_ref, f1_ref, join_ref):
    for ref in (dconv_ref, dout_ref, hsum_ref, rsum_ref, grad_ref, d_ref.at[2], act_ref.at[2], low_ref.at[1]):
        ref[...] = jnp.zeros(ref.shape, ref.dtype)
    zero = jnp.zeros((8, 128), F32)
    for ref in (f0_ref, f1_ref):
        ref[0:8, :] = zero
        ref[8 * PX + 8:8 * PX + 16, :] = zero
    join_ref[20:24, :] = jnp.zeros((4, PLANE), F32)


def mark(labels_ref, hot_ref, scale):
    bins = iota((BINS, TILE), 0)

    def body(row, carry):
        for k in range(PLANE // TILE):
            cols = slice(TILE * k, TILE * k + TILE)
            hot_ref[row, :, cols] = jnp.where(bins == labels_ref[pl.ds(row, 1), cols], scale, 0.0)
        return carry

    lax.fori_loop(0, PX, body, 0)


def train(hot_ref, early_ref, wide_ref, owt_ref, owb_ref, g_ref, act_ref, d_ref, low_ref, grad_ref, z_ref, pick_ref, dconv_ref, dout_ref, hsum_ref, rsum_ref, scale):
    ones = jnp.ones((16, TILE), BF16)
    width = CH * TILE
    per = PLANE // width
    steps = NB * per
    tiles = [(c, x) for c in range(CH) for x in range(XB)]

    def span(c):
        return slice(c * TILE, (c + 1) * TILE)

    def place(step, c):
        return step // per, pl.ds(pl.multiple_of((step % per) * width + c * TILE, TILE), TILE)

    def within(step):
        return jnp.clip(step, 0, steps - 1)

    def hidden_dot(step, c):
        b, cols = place(within(step), c)
        return jnp.dot(wide_ref[...], g_ref[b, :, cols], preferred_element_type=F32)

    def silu(step, c, x, u_all):
        slot = lax.rem(step, 3)
        u = u_all[x * HID:(x + 1) * HID]
        t = jnp.tanh(u)
        w = 1.0 + t
        a = u * w
        act_ref[slot, x, :, span(c)] = a.astype(BF16)
        d_ref[slot, x, :, span(c)] = (w + a) - a * t

    def hidden(step):
        for c in range(CH):
            u_all = hidden_dot(step, c)
            for x in range(XB):
                silu(step, c, x, u_all)

    def logit(step, c, x):
        slot = lax.rem(step, 3)
        return jnp.dot(owt_ref[...], jnp.concatenate([act_ref[slot, x, :, span(c)], ones], axis=0), preferred_element_type=F32)

    def softmax(step, c, x, logits):
        b, cols = place(step, c)
        row = XB * b + x
        e = jnp.exp(logits)
        hot = hot_ref[row, :, cols]
        picked = logits * hot
        picked = sum(picked[8 * k:8 * k + 8] for k in range(BINS // 8))
        for half in range(TILE // 128):
            lane = (step % per) * (width // 128) + c * (TILE // 128) + half
            pick_ref[lane, pl.ds(pl.multiple_of(8 * row, 8), 8), :] = picked[:, 128 * half:128 * half + 128]
        total = jnp.sum(e, axis=0, keepdims=True)
        z_ref[pl.ds(row, 1), cols] = total
        r = e * (scale / total) - hot
        low_ref[lax.rem(step, 2), x, :, span(c)] = r.astype(BF16)
        return fold(r)

    def back(step, c, x):
        prod = jnp.dot(owb_ref[...], low_ref[lax.rem(step, 2), x, :, span(c)], preferred_element_type=F32)
        grad = prod * d_ref[lax.rem(step, 3), x, :, span(c)]
        grad_ref[lax.rem(step, 2), x * HID:(x + 1) * HID, span(c)] = grad.astype(BF16)
        return fold(grad)

    def out_grad(step, part, parts):
        xs = range(part * XB // parts, (part + 1) * XB // parts)
        dout_ref[...] += lax.dot_general(
            jnp.concatenate([act_ref[lax.rem(step, 3), x] for x in xs], axis=1),
            jnp.concatenate([low_ref[lax.rem(step, 2), x] for x in xs], axis=1), NT, preferred_element_type=F32)

    def conv_grad(step, at, part, parts):
        b = at // per
        cols = pl.ds(pl.multiple_of((at % per) * width, width), width)
        rows = slice(part * XB * HID // parts, (part + 1) * XB * HID // parts)
        dconv_ref[rows, :] += lax.dot_general(grad_ref[lax.rem(step, 2), rows, :], g_ref[b, :, cols], NT, preferred_element_type=F32)

    def add(total, term):
        return term if total is None else total + term

    hidden(0)
    for i in range(LEAD):
        early_ref[i] = logit(0, *tiles[i])

    def body(step, carry):
        old, oldest, ahead = step + 5, step + 4, step + 1
        hsum = rsum = None
        logits = {t: early_ref[i] for i, t in enumerate(tiles[:LEAD])}
        n = len(tiles)
        u_all = {}
        for i, t in enumerate(tiles):
            if i in HIDDEN_AT:
                u_all[HIDDEN_AT.index(i)] = hidden_dot(ahead, HIDDEN_AT.index(i))
            hsum = add(hsum, back(old, *t))
            if i in CONV_AT:
                conv_grad(oldest, within(step - 2), CONV_AT.index(i), len(CONV_AT))
            if i in OUT_AT:
                out_grad(old, OUT_AT.index(i), len(OUT_AT))
            if i + LEAD < n:
                logits[tiles[i + LEAD]] = logit(step, *tiles[i + LEAD])
            silu(ahead, *t, u_all[t[0]])
            rsum = add(rsum, softmax(step, *t, logits.pop(t)))
        for i in range(LEAD):
            early_ref[i] = logit(ahead, *tiles[i])
        rsum_ref[...] += rsum
        hsum_ref[...] += hsum
        return carry

    lax.fori_loop(0, steps, body, 0)
    hsum = None
    for t in tiles:
        hsum = add(hsum, back(steps - 1, *t))
    hsum_ref[...] += hsum
    for k in range(2):
        conv_grad(steps - 1, steps - 1, k, 2)
        conv_grad(steps - 2, steps - 2, k, 2)
    out_grad(steps - 1, 0, 1)


def losses(z_ref, pick_ref, loss_ref, scale):
    for lane in range(PLANE // 128):
        cols = slice(128 * lane, 128 * lane + 128)
        picked = sum(pick_ref[lane, pl.ds(k, PX, stride=8), :] for k in range(8))
        loss_ref[:, cols] = jnp.log(z_ref[:, cols]) - picked / scale


def finish(dconv_ref, dout_ref, hsum_ref, rsum_ref, part_ref):
    total = dconv_ref[0:HID, :]
    for x in range(1, XB):
        total = total + pltpu.roll(dconv_ref[x * HID:(x + 1) * HID, :], KP - x, 1)
    col = iota((HID, KP), 1)
    hcol = jnp.sum(hsum_ref[...], axis=1, keepdims=True)
    rcol = jnp.sum(rsum_ref[...], axis=1, keepdims=True)
    total = jnp.where(col == KC, hcol, jnp.where(col == KC + 1, rcol, total))
    k, c = iota((HID, KP), 0), iota((HID, KP), 1)
    pick = conv_rows(0, (HID, KP), 0, 1) | ((k == FEATS) & (c == KC)) | ((k == FEATS + 1) & (c == KC + 1))
    rows = lax.dot_general(jnp.where(pick, 1.0, 0.0), total, NT, precision=lax.Precision.HIGHEST, preferred_element_type=F32)
    part_ref[:, 0:HID] = rows
    part_ref[:, HID:2 * HID] = dout_ref[...]


def compute_scratch():
    return [
        pltpu.VMEM((8 * PX + 16, 128), F32), pltpu.VMEM((8 * PX + 16, 128), F32),
        pltpu.VMEM((GROUP, PLANE), F32),
        pltpu.VMEM((NB, KP, PLANE), BF16),
        pltpu.VMEM((XB * HID, KP), BF16), pltpu.VMEM((BINS, KO), BF16), pltpu.VMEM((HID, BINS), BF16),
        pltpu.VMEM((3, XB, HID, CH * TILE), BF16), pltpu.VMEM((3, XB, HID, CH * TILE), F32),
        pltpu.VMEM((2, XB, BINS, CH * TILE), BF16), pltpu.VMEM((2, XB * HID, CH * TILE), BF16), pltpu.VMEM((PX, BINS, PLANE), F32), pltpu.VMEM((LEAD, BINS, TILE), F32),
        pltpu.VMEM((XB * HID, KP), F32), pltpu.VMEM((HID, BINS), F32),
        pltpu.VMEM((HID, 128), F32), pltpu.VMEM((BINS, 128), F32),
    ]


SEC, SP, YHI, Z = 4, 8, 2, 12
TEAM = SEC * SP
Y = SEC * YHI
ROWS = HID // SP
SCALE = 1.0 / 25165824
MESH = pl.DeviceIdType.MESH


def place_here():
    sec, sp, dp = lax.axis_index("sec"), lax.axis_index("sp"), lax.axis_index("dp")
    return sec, sp, dp // Z, lax.rem(dp, Z)


def flips(value):
    return value, value + 1 - 2 * lax.rem(value, 2), lax.rem(value + 2, 4), 3 - value


def sp_flips(sp):
    chips, core = flips(sp // 2), lax.rem(sp, 2)
    return [2 * chips[k // 2] + (1 - core if k % 2 else core) for k in range(SP)]


CHIP_HOPS = (0, 1, 2, 1)
SP_FAR = sorted(range(1, SP), key=lambda k: -CHIP_HOPS[k // 2])
TEAM_FAR = sorted(((a, k) for a in range(SEC) for k in range(SP) if a or k), key=lambda t: -t[0] - CHIP_HOPS[t[1] // 2])
Y_FAR = [(1, a) for a in (3, 2, 1, 0)] + [(0, a) for a in (3, 2, 1)]


def rings():
    sec, sp, yhi, z = place_here()
    secs, sps = flips(sec), sp_flips(sp)
    team = [(secs[a] * SP + sps[k], {"sec": secs[a], "sp": sps[k]}) for a, k in TEAM_FAR]
    row = [(sps[k], {"sp": sps[k]}) for k in SP_FAR]
    across = ((yhi, yhi * Z + z), (1 - yhi, (1 - yhi) * Z + z))
    ys = [(across[f][0] * SEC + secs[a], {"sec": secs[a], "dp": across[f][1]}) for f, a in Y_FAR]
    zs = []
    for i in sorted(range(1, Z), key=lambda i: -min(i, Z - i)):
        other = jnp.where(z + i >= Z, z + i - Z, z + i)
        zs.append((other, {"dp": yhi * Z + other}))
    return team, row, ys, zs


def greet(*groups):
    barrier = pltpu.get_barrier_semaphore()
    count = 0
    for group in groups:
        for _, device in group:
            pl.semaphore_signal(barrier, inc=1, device_id=device, device_id_type=MESH)
            count += 1
    pl.semaphore_wait(barrier, count)


def remote(src, dst, send_sem, recv_sem, device):
    return pltpu.make_async_remote_copy(
        src_ref=src, dst_ref=dst, send_sem=send_sem, recv_sem=recv_sem, device_id=device, device_id_type=MESH)


def relay(team, frac_ref, patch_ref, send_sem, recv_sem):
    sec, sp, _, _ = place_here()
    spot = patch_ref.at[sp, pl.ds(pl.multiple_of(8 * sec, 8), 8), :]
    for rank, device in team:
        remote(frac_ref.at[rank], spot, send_sem, recv_sem, device).start()
    pltpu.make_async_copy(frac_ref.at[sec * SP + sp], spot, recv_sem).start()

    def arrive():
        pltpu.make_async_copy(patch_ref, patch_ref, recv_sem).wait()

    def leave():
        sent = frac_ref.at[pl.ds(0, TEAM - 1)]
        remote(sent, sent, send_sem, recv_sem, team[0][1]).wait_send()

    return arrive, leave


def post(ring, me, source, slots, send_sem, recv_sem):
    for rank, device in ring:
        remote(source(rank), slots.at[me], send_sem, recv_sem, device).start()
    others = slots.at[pl.ds(0, len(ring))]
    both = remote(others, others, send_sem, recv_sem, ring[0][1])
    return both.wait_recv, both.wait_send


def reduce_grads(meanwhile, row, ys, zs, part, first, yslots, zslots, pieces, total, result_ref, sends, recvs):
    sec, sp, yhi, z = place_here()
    y = yhi * SEC + sec
    half = ROWS // 2
    leaves = []

    def rows(rank):
        return part.at[pl.ds(pl.multiple_of(rank * ROWS, ROWS), ROWS), :]

    def share(ring, me, value, k, slots):
        pieces[k] = value
        slots[me] = value
        take, leave = post(ring, me, lambda rank: pieces.at[k], slots, sends.at[k], recvs.at[k])
        leaves.append(leave)
        return take

    first[sp] = rows(sp)[...]
    take, leave = post(row, sp, rows, first, sends.at[4], recvs.at[4])
    leaves.append(leave)
    take()
    both = jnp.sum(first[...], axis=0)
    take_z = share(zs, z, both[half:], 1, zslots.at[1])
    take_y = share(ys, y, both[:half], 0, yslots.at[0])
    take_y()
    last_z = share(zs, z, jnp.sum(yslots[0], axis=0), 2, zslots.at[0])
    take_z()
    last_y = share(ys, y, jnp.sum(zslots[1], axis=0), 3, yslots.at[1])
    meanwhile()
    last_y()
    total[half:, :] = jnp.sum(yslots[1], axis=0)
    last_z()
    total[:half, :] = jnp.sum(zslots[0], axis=0)
    mine = pltpu.make_async_copy(total, result_ref.at[sp], sends.at[5])
    mine.start()
    take, leave = post(row, sp, lambda rank: total, result_ref, sends.at[6], recvs.at[5])
    take()
    return leaves + [leave, mine.wait]


def step_kernel(frac_ref, labels_ref, cw_ref, cb_ref, ow_ref, ob_ref, grads_ref, loss_ref,
                z, pick, loss, out_sem, patch, labels, cw, cb, ow, ob, in_sems, send_sems, recv_sems,
                part, first, yslots, zslots, pieces, total,
                f0, f1, join, g, wide, owt, owb, act, d, low, grad, hot, early, dconv, dout, hsum, rsum):
    loads = [pltpu.make_async_copy(src, dst, in_sems.at[i]) for i, (src, dst) in enumerate(
        ((cw_ref, cw), (cb_ref, cb), (ow_ref, ow), (ob_ref, ob), (labels_ref, labels)))]
    for load in loads:
        load.start()
    team, row, ys, zs = rings()
    greet(team, zs, ys[:SEC])
    arrive, leave = relay(team, frac_ref, patch, send_sems.at[7], recv_sems.at[6])
    for load in loads:
        load.wait()
    prepare(cw, cb, ow, ob, wide, owt, owb)
    clear(d, act, low, grad, dconv, dout, hsum, rsum, f0, f1, join)
    mark(labels, hot, SCALE)
    arrive()
    filter_patch(patch, f0, f1)
    stencil(f0, f1, join, g)
    train(hot, early, wide, owt, owb, g, act, d, low, grad, z, pick, dconv, dout, hsum, rsum, SCALE)
    finish(dconv, dout, hsum, rsum, part)

    def save_loss():
        losses(z, pick, loss, SCALE)
        pltpu.make_async_copy(loss, loss_ref, out_sem).start()

    leaves = reduce_grads(save_loss, row, ys, zs, part, first, yslots, zslots, pieces, total, grads_ref, send_sems, recv_sems)
    for end in [leave] + leaves:
        end()
    pltpu.make_async_copy(loss, loss_ref, out_sem).wait()


def train_step(frac, labels, cw, cb, ow, ob):
    far = pl.BlockSpec(memory_space=pl.ANY)
    dma = pltpu.SemaphoreType.DMA
    plane = pltpu.VMEM((PX, PLANE), F32)
    return pl.pallas_call(
        step_kernel,
        out_shape=(jax.ShapeDtypeStruct((SP, ROWS, 128), F32), jax.ShapeDtypeStruct((PX, PLANE), F32)),
        in_specs=[far] * 6,
        out_specs=(far, far),
        scratch_shapes=[
            plane, pltpu.VMEM((PLANE // 128, 8 * PX, 128), F32), plane, dma,
            pltpu.VMEM((SP, 8 * SEC, 128), F32), pltpu.VMEM((PX, PLANE), jnp.int32),
            pltpu.VMEM((FEATS, HID), BF16), pltpu.VMEM((HID,), F32), pltpu.VMEM((HID, BINS), BF16), pltpu.VMEM((BINS,), F32),
            dma((5,)), dma((8,)), dma((7,)),
            pltpu.VMEM((HID, 128), F32), pltpu.VMEM((SP, ROWS, 128), F32), pltpu.VMEM((2, Y, ROWS // 2, 128), F32),
            pltpu.VMEM((2, Z, ROWS // 2, 128), F32), pltpu.VMEM((4, ROWS // 2, 128), F32), pltpu.VMEM((ROWS, 128), F32),
        ] + compute_scratch(),
        compiler_params=pltpu.CompilerParams(collective_id=0, has_side_effects=True, vmem_limit_bytes=56 * 2**20),
        name="train_step",
    )(frac, labels, cw, cb, ow, ob)


def close_kernel(grads_ref, loss_in, loss_ref, conv_ref, cbias_ref, out_ref, obias_ref, grads, sems):
    loss = pltpu.make_async_copy(loss_in, loss_ref, sems.at[0])
    load = pltpu.make_async_copy(grads_ref, grads, sems.at[1])
    load.start()
    loss.start()
    load.wait()
    full = jnp.concatenate([grads[i] for i in range(SP)], axis=0)
    conv_ref[...] = full[:FEATS, :HID]
    cbias_ref[...] = full[FEATS:FEATS + 1, :HID].reshape(HID)
    obias_ref[...] = full[FEATS + 1:FEATS + 2, :HID].reshape(BINS)
    out_ref[...] = full[:, HID:]
    loss.wait()


def close(grads, loss):
    vm, far = pl.BlockSpec(memory_space=pltpu.VMEM), pl.BlockSpec(memory_space=pl.ANY)
    return pl.pallas_call(
        close_kernel,
        out_shape=(jax.ShapeDtypeStruct((PX, PLANE), F32), jax.ShapeDtypeStruct((FEATS, HID), F32),
                   jax.ShapeDtypeStruct((HID,), F32), jax.ShapeDtypeStruct((HID, BINS), F32),
                   jax.ShapeDtypeStruct((BINS,), F32)),
        in_specs=[far, far],
        out_specs=(vm, vm, vm, vm, vm),
        scratch_shapes=[pltpu.VMEM((SP, ROWS, 128), F32), pltpu.SemaphoreType.DMA((2,))],
        compiler_params=pltpu.CompilerParams(vmem_limit_bytes=56 * 2**20),
        name="close_step",
    )(grads, loss)


def shards(fraction, labels, conv_weight, conv_bias, out_weight, out_bias):
    blocks = fraction.reshape(TEAM, 4, 2, 128).transpose(0, 2, 1, 3).reshape(TEAM, 8, 128)
    grads, loss = train_step(blocks, labels.reshape(PX, PLANE),
                             conv_weight, conv_bias, out_weight, out_bias)
    loss, conv, cbias, out, obias = close(grads, loss)
    return loss.reshape(labels.shape), conv, cbias, out, obias


def solution(mesh):
    placed = (P("dp", None, "sp", "sec"), P("dp", ("sec", "sp"), None, None), P(), P(), P(), P())
    return jax.shard_map(
        shards,
        mesh=mesh,
        in_specs=placed,
        out_specs=(P("dp", ("sec", "sp"), None, None), P(), P(), P(), P()),
        check_vma=False,
    )
```

```python
import functools
import jax
import jax.numpy as jnp
from jax import lax
from jax.experimental import pallas as pl
from jax.experimental.pallas import tpu as pltpu
from jax.sharding import PartitionSpec as P

PX, PY, PZ = 32, 32, 32
PLANE = PY * PZ
HID = 64
BINS = 64
FEATS = 54
XB = 8
NB = PX // XB
GROUP = 24
KC = 9 * GROUP
KP = KC + 8
KO = HID + 16
TILE = 256
F32, BF16 = jnp.float32, jnp.bfloat16
LEAD = 2
CH = 2
HIDDEN_AT = (0, 4)
CONV_AT = (1, 3)
OUT_AT = (5, 7, 9, 11)
NT = (((1,), (1,)), ((), ()))
TN = (((0,), (0,)), ((), ()))


def iota(shape, axis):
    return lax.broadcasted_iota(jnp.int32, shape, axis)


def split3(value):
    high = value.astype(BF16)
    rest = value - high.astype(F32)
    mid = rest.astype(BF16)
    low = (rest - mid.astype(F32)).astype(BF16)
    return high.astype(F32), mid.astype(F32), low.astype(F32)


def column(row):
    n = row.shape[1]
    eye = iota((n, n), 0) == iota((n, n), 1)
    return jnp.sum(jnp.where(eye, row, 0.0), axis=1, keepdims=True)


def conv_rows(p_minus_x, shape, k_axis, c_axis):
    col = iota(shape, c_axis)
    k = iota(shape, k_axis)
    t = col // GROUP
    u = col - t * GROUP
    c = jnp.where(u >= 10, 1, 0)
    dx = u - 10 * c - p_minus_x
    return (col < KC) & (u < 20) & (dx >= 0) & (dx < 3) & (k == 18 * dx + 2 * t + c)


def prepare(cw_ref, cb_ref, ow_ref, ob_ref, wide_ref, owt_ref, owb_ref):
    cb = column(cb_ref[...].reshape(1, HID)) * 0.5
    ch, cm, cl = split3(cb)
    col = iota((HID, KP), 1)
    bias = jnp.where(col == KC, ch, jnp.where(col == KC + 1, cm, jnp.where(col == KC + 2, cl, 0.0)))
    cw = cw_ref[...]
    for x in range(XB):
        pick = jnp.where(conv_rows(x, (FEATS, KP), 0, 1), 0.5, 0.0).astype(BF16)
        row = lax.dot_general(cw, pick, TN, preferred_element_type=F32) + bias
        wide_ref[x * HID:(x + 1) * HID, :] = row.astype(BF16)
    ob = column(ob_ref[...].reshape(1, BINS))
    oh, om, ol = split3(ob)
    ow = ow_ref[...]
    eye = (iota((HID, KO), 0) == iota((HID, KO), 1)).astype(F32).astype(BF16)
    owt = lax.dot_general(ow, eye, TN, preferred_element_type=F32)
    col = iota((BINS, KO), 1)
    owt = owt + jnp.where(col == HID, oh, jnp.where(col == HID + 1, om, jnp.where(col == HID + 2, ol, 0.0)))
    owt_ref[...] = owt.astype(BF16)
    owb_ref[...] = (ow.astype(F32) * 0.5).astype(BF16)


def shift_z(parts, step):
    z = iota(parts[0].shape, 1) & (PZ - 1)
    edge = z == (0 if step > 0 else PZ - 1)
    return [jnp.where(edge, 0.0, pltpu.roll(part, step % 128, 1)) for part in parts]


def rows_wrap(step):
    lane = iota((8, 128), 1)
    return lane < PZ if step > 0 else lane >= 128 - PZ


def shift_y(parts, step):
    wraps = jnp.broadcast_to(rows_wrap(step)[0:1], parts[0].shape)
    rolled = [pltpu.roll(part, step * PZ % 128, 1) for part in parts]
    ends = [jnp.zeros_like(parts[0])]
    near = ends + rolled[:-1] if step > 0 else rolled[1:] + ends
    return [jnp.where(wraps, other, own) for other, own in zip(near, rolled)]


def box(planes):
    none = [jnp.zeros_like(planes[0])]
    s = [a + b + c for a, b, c in zip(none + planes[:-1], planes, planes[1:] + none)]
    s = [mid + lo + hi for mid, lo, hi in zip(s, shift_z(s, 1), shift_z(s, -1))]
    group = iota((8, 128), 0)
    sums = []
    for v in s:
        for step, last in ((1, 0), (-1, 7)):
            rolled = pltpu.roll(v, step * PZ % 128, 1)
            near = jnp.where(group == last, 0.0, pltpu.roll(rolled, step % 8, 0))
            sums.append(jnp.where(rows_wrap(step), near, rolled))
    return [(v + sums[2 * k] + sums[2 * k + 1]) / 27.0 for k, v in enumerate(s)]


def filter_patch(patch_ref, f0_ref, f1_ref):
    planes = [patch_ref[p // 4, pl.ds(p % 4, 8, stride=4), :] for p in range(PX)]
    filt = box(planes)
    square = box([p * p for p in planes])
    for p in range(PX):
        rows = slice(8 * p + 8, 8 * p + 16)
        f0_ref[rows, :] = filt[p]
        f1_ref[rows, :] = square[p] - filt[p] * filt[p]


def stencil(f0_ref, f1_ref, join_ref, g_ref):
    ones = jnp.ones((8, 128), F32)
    for b in range(NB):
        mid = []
        for k in range(PLANE // 128):
            cols = slice(128 * k, 128 * k + 128)
            join_ref[0:10, cols] = f0_ref[pl.ds(64 * b + k, 10, stride=8), :]
            join_ref[10:20, cols] = f1_ref[pl.ds(64 * b + k, 10, stride=8), :]
            mid.append(join_ref[:, cols])
        taps = []
        for step_y in (1, 0, -1):
            row = shift_y(mid, step_y) if step_y else mid
            taps += [shift_z(row, 1), row, shift_z(row, -1)]
        for k in range(PLANE // 128):
            rows = jnp.concatenate([tap[k] for tap in taps] + [ones], axis=0)
            g_ref[b, :, 128 * k:128 * k + 128] = rows.astype(BF16)


def fold(v):
    return v[:, :128] + v[:, 128:]


def clear(d_ref, act_ref, low_ref, grad_ref, dconv_ref, dout_ref, hsum_ref, rsum_ref, f0_ref, f1_ref, join_ref):
    for ref in (dconv_ref, dout_ref, hsum_ref, rsum_ref, grad_ref, d_ref.at[2], act_ref.at[2], low_ref.at[1]):
        ref[...] = jnp.zeros(ref.shape, ref.dtype)
    zero = jnp.zeros((8, 128), F32)
    for ref in (f0_ref, f1_ref):
        ref[0:8, :] = zero
        ref[8 * PX + 8:8 * PX + 16, :] = zero
    join_ref[20:24, :] = jnp.zeros((4, PLANE), F32)


def mark(labels_ref, hot_ref, scale):
    bins = iota((BINS, TILE), 0)

    def body(row, carry):
        for k in range(PLANE // TILE):
            cols = slice(TILE * k, TILE * k + TILE)
            hot_ref[row, :, cols] = jnp.where(bins == labels_ref[pl.ds(row, 1), cols], scale, 0.0)
        return carry

    lax.fori_loop(0, PX, body, 0)


def train(hot_ref, early_ref, wide_ref, owt_ref, owb_ref, g_ref, act_ref, d_ref, low_ref, grad_ref, z_ref, pick_ref, dconv_ref, dout_ref, hsum_ref, rsum_ref, scale):
    ones = jnp.ones((16, TILE), BF16)
    width = CH * TILE
    per = PLANE // width
    steps = NB * per
    tiles = [(c, x) for c in range(CH) for x in range(XB)]

    def span(c):
        return slice(c * TILE, (c + 1) * TILE)

    def place(step, c):
        return step // per, pl.ds(pl.multiple_of((step % per) * width + c * TILE, TILE), TILE)

    def within(step):
        return jnp.clip(step, 0, steps - 1)

    def hidden_dot(step, c):
        b, cols = place(within(step), c)
        return jnp.dot(wide_ref[...], g_ref[b, :, cols], preferred_element_type=F32)

    def silu(step, c, x, u_all):
        slot = lax.rem(step, 3)
        u = u_all[x * HID:(x + 1) * HID]
        t = jnp.tanh(u)
        w = 1.0 + t
        a = u * w
        act_ref[slot, x, :, span(c)] = a.astype(BF16)
        d_ref[slot, x, :, span(c)] = (w + a) - a * t

    def hidden(step):
        for c in range(CH):
            u_all = hidden_dot(step, c)
            for x in range(XB):
                silu(step, c, x, u_all)

    def logit(step, c, x):
        slot = lax.rem(step, 3)
        return jnp.dot(owt_ref[...], jnp.concatenate([act_ref[slot, x, :, span(c)], ones], axis=0), preferred_element_type=F32)

    def softmax(step, c, x, logits):
        b, cols = place(step, c)
        row = XB * b + x
        e = jnp.exp(logits)
        hot = hot_ref[row, :, cols]
        picked = logits * hot
        picked = sum(picked[8 * k:8 * k + 8] for k in range(BINS // 8))
        for half in range(TILE // 128):
            lane = (step % per) * (width // 128) + c * (TILE // 128) + half
            pick_ref[lane, pl.ds(pl.multiple_of(8 * row, 8), 8), :] = picked[:, 128 * half:128 * half + 128]
        total = jnp.sum(e, axis=0, keepdims=True)
        z_ref[pl.ds(row, 1), cols] = total
        r = e * (scale / total) - hot
        low_ref[lax.rem(step, 2), x, :, span(c)] = r.astype(BF16)
        return fold(r)

    def back(step, c, x):
        prod = jnp.dot(owb_ref[...], low_ref[lax.rem(step, 2), x, :, span(c)], preferred_element_type=F32)
        grad = prod * d_ref[lax.rem(step, 3), x, :, span(c)]
        grad_ref[lax.rem(step, 2), x * HID:(x + 1) * HID, span(c)] = grad.astype(BF16)
        return fold(grad)

    def out_grad(step, part, parts):
        xs = range(part * XB // parts, (part + 1) * XB // parts)
        dout_ref[...] += lax.dot_general(
            jnp.concatenate([act_ref[lax.rem(step, 3), x] for x in xs], axis=1),
            jnp.concatenate([low_ref[lax.rem(step, 2), x] for x in xs], axis=1), NT, preferred_element_type=F32)

    def conv_grad(step, at, part, parts):
        b = at // per
        cols = pl.ds(pl.multiple_of((at % per) * width, width), width)
        rows = slice(part * XB * HID // parts, (part + 1) * XB * HID // parts)
        dconv_ref[rows, :] += lax.dot_general(grad_ref[lax.rem(step, 2), rows, :], g_ref[b, :, cols], NT, preferred_element_type=F32)

    def add(total, term):
        return term if total is None else total + term

    hidden(0)
    for i in range(LEAD):
        early_ref[i] = logit(0, *tiles[i])

    def body(step, carry):
        old, oldest, ahead = step + 5, step + 4, step + 1
        hsum = rsum = None
        logits = {t: early_ref[i] for i, t in enumerate(tiles[:LEAD])}
        n = len(tiles)
        u_all = {}
        for i, t in enumerate(tiles):
            if i in HIDDEN_AT:
                u_all[HIDDEN_AT.index(i)] = hidden_dot(ahead, HIDDEN_AT.index(i))
            hsum = add(hsum, back(old, *t))
            if i in CONV_AT:
                conv_grad(oldest, within(step - 2), CONV_AT.index(i), len(CONV_AT))
            if i in OUT_AT:
                out_grad(old, OUT_AT.index(i), len(OUT_AT))
            if i + LEAD < n:
                logits[tiles[i + LEAD]] = logit(step, *tiles[i + LEAD])
            silu(ahead, *t, u_all[t[0]])
            rsum = add(rsum, softmax(step, *t, logits.pop(t)))
        for i in range(LEAD):
            early_ref[i] = logit(ahead, *tiles[i])
        rsum_ref[...] += rsum
        hsum_ref[...] += hsum
        return carry

    lax.fori_loop(0, steps, body, 0)
    hsum = None
    for t in tiles:
        hsum = add(hsum, back(steps - 1, *t))
    hsum_ref[...] += hsum
    for k in range(2):
        conv_grad(steps - 1, steps - 1, k, 2)
        conv_grad(steps - 2, steps - 2, k, 2)
    out_grad(steps - 1, 0, 1)


def losses(z_ref, pick_ref, loss_ref, scale):
    for lane in range(PLANE // 128):
        cols = slice(128 * lane, 128 * lane + 128)
        picked = sum(pick_ref[lane, pl.ds(k, PX, stride=8), :] for k in range(8))
        loss_ref[:, cols] = jnp.log(z_ref[0:PX, cols]) - picked / scale


def finish(dconv_ref, dout_ref, hsum_ref, rsum_ref, part_ref):
    total = dconv_ref[0:HID, :]
    for x in range(1, XB):
        total = total + pltpu.roll(dconv_ref[x * HID:(x + 1) * HID, :], KP - x, 1)
    col = iota((HID, KP), 1)
    hcol = jnp.sum(hsum_ref[...], axis=1, keepdims=True)
    rcol = jnp.sum(rsum_ref[...], axis=1, keepdims=True)
    total = jnp.where(col == KC, hcol, jnp.where(col == KC + 1, rcol, total))
    k, c = iota((HID, KP), 0), iota((HID, KP), 1)
    pick = conv_rows(0, (HID, KP), 0, 1) | ((k == FEATS) & (c == KC)) | ((k == FEATS + 1) & (c == KC + 1))
    rows = lax.dot_general(jnp.where(pick, 1.0, 0.0), total, NT, precision=lax.Precision.HIGHEST, preferred_element_type=F32)
    part_ref[:, 0:HID] = rows
    part_ref[:, HID:2 * HID] = dout_ref[...]


def compute_scratch():
    return [
        pltpu.VMEM((8 * PX + 80, 128), F32), pltpu.VMEM((8 * PX + 80, 128), F32),
        pltpu.VMEM((GROUP, PLANE), F32),
        pltpu.VMEM((NB, KP, PLANE), BF16),
        pltpu.VMEM((XB * HID, KP), BF16), pltpu.VMEM((BINS, KO), BF16), pltpu.VMEM((HID, BINS), BF16),
        pltpu.VMEM((3, XB, HID, CH * TILE), BF16), pltpu.VMEM((3, XB, HID, CH * TILE), F32),
        pltpu.VMEM((2, XB, BINS, CH * TILE), BF16), pltpu.VMEM((2, XB * HID, CH * TILE), BF16), pltpu.VMEM((PX, BINS, PLANE), F32), pltpu.VMEM((LEAD, BINS, TILE), F32),
        pltpu.VMEM((XB * HID, KP), F32), pltpu.VMEM((HID, BINS), F32),
        pltpu.VMEM((HID, 128), F32), pltpu.VMEM((BINS, 128), F32),
    ]


SEC, SP, YHI, Z = 4, 8, 2, 12
TEAM = SEC * SP
Y = SEC * YHI
ROWS = HID // SP
SCALE = 1.0 / 25165824
MESH = pl.DeviceIdType.MESH


def place_here():
    sec, sp, dp = lax.axis_index("sec"), lax.axis_index("sp"), lax.axis_index("dp")
    return sec, sp, dp // Z, lax.rem(dp, Z)


def flips(value):
    return value, value + 1 - 2 * lax.rem(value, 2), lax.rem(value + 2, 4), 3 - value


def sp_flips(sp):
    chips, core = flips(sp // 2), lax.rem(sp, 2)
    return [2 * chips[k // 2] + (1 - core if k % 2 else core) for k in range(SP)]


CHIP_HOPS = (0, 1, 2, 1)
SP_FAR = sorted(range(1, SP), key=lambda k: -CHIP_HOPS[k // 2])
TEAM_FAR = sorted(((a, k) for a in range(SEC) for k in range(SP) if a or k), key=lambda t: -t[0] - CHIP_HOPS[t[1] // 2])
Y_FAR = [(1, a) for a in (3, 2, 1, 0)] + [(0, a) for a in (3, 2, 1)]


def rings():
    sec, sp, yhi, z = place_here()
    secs, sps = flips(sec), sp_flips(sp)
    team = [(secs[a] * SP + sps[k], {"sec": secs[a], "sp": sps[k]}) for a, k in TEAM_FAR]
    row = [(sps[k], {"sp": sps[k]}) for k in SP_FAR]
    across = ((yhi, yhi * Z + z), (1 - yhi, (1 - yhi) * Z + z))
    ys = [(across[f][0] * SEC + secs[a], {"sec": secs[a], "dp": across[f][1]}) for f, a in Y_FAR]
    zs = []
    for i in sorted(range(1, Z), key=lambda i: -min(i, Z - i)):
        other = jnp.where(z + i >= Z, z + i - Z, z + i)
        zs.append((other, {"dp": yhi * Z + other}))
    return team, row, ys, zs


def greet(loads, *groups):
    barrier = pltpu.get_barrier_semaphore()
    count = 0
    for group in groups:
        for _, device in group:
            pl.semaphore_signal(barrier, inc=1, device_id=device, device_id_type=MESH)
            count += 1
    for load in loads:
        load.start()
    pl.semaphore_wait(barrier, count)


def remote(src, dst, send_sem, recv_sem, device):
    return pltpu.make_async_remote_copy(
        src_ref=src, dst_ref=dst, send_sem=send_sem, recv_sem=recv_sem, device_id=device, device_id_type=MESH)


def relay(team, frac_ref, patch_ref, send_sem, recv_sem):
    sec, sp, _, _ = place_here()
    spot = patch_ref.at[sp, pl.ds(pl.multiple_of(8 * sec, 8), 8), :]
    for rank, device in team:
        remote(frac_ref.at[rank], spot, send_sem, recv_sem, device).start()
    pltpu.make_async_copy(frac_ref.at[sec * SP + sp], spot, recv_sem).start()

    def arrive():
        pltpu.make_async_copy(patch_ref, patch_ref, recv_sem).wait()

    def leave():
        sent = frac_ref.at[pl.ds(0, TEAM - 1)]
        remote(sent, sent, send_sem, recv_sem, team[0][1]).wait_send()

    return arrive, leave


def post(ring, me, source, slots, send_sem, recv_sem):
    for rank, device in ring:
        remote(source(rank), slots.at[me], send_sem, recv_sem, device).start()
    others = slots.at[pl.ds(0, len(ring))]
    both = remote(others, others, send_sem, recv_sem, ring[0][1])
    return both.wait_recv, both.wait_send


def reduce_grads(meanwhile, row, ys, zs, part, first, yslots, zslots, pieces, total, result_ref, sends, recvs):
    sec, sp, yhi, z = place_here()
    y = yhi * SEC + sec
    half = ROWS // 2
    leaves = []

    def rows(rank):
        return part.at[pl.ds(pl.multiple_of(rank * ROWS, ROWS), ROWS), :]

    def share(ring, me, value, k, slots):
        pieces[k] = value
        slots[me] = value
        take, leave = post(ring, me, lambda rank: pieces.at[k], slots, sends.at[k], recvs.at[k])
        leaves.append(leave)
        return take

    first[sp] = rows(sp)[...]
    take, leave = post(row, sp, rows, first, sends.at[4], recvs.at[4])
    leaves.append(leave)
    take()
    both = jnp.sum(first[...], axis=0)
    take_z = share(zs, z, both[half:], 1, zslots.at[1])
    take_y = share(ys, y, both[:half], 0, yslots.at[0])
    take_y()
    last_z = share(zs, z, jnp.sum(yslots[0], axis=0), 2, zslots.at[0])
    take_z()
    last_y = share(ys, y, jnp.sum(zslots[1], axis=0), 3, yslots.at[1])
    meanwhile()
    last_y()
    total[half:, :] = jnp.sum(yslots[1], axis=0)
    last_z()
    total[:half, :] = jnp.sum(zslots[0], axis=0)
    mine = pltpu.make_async_copy(total, result_ref.at[sp], sends.at[5])
    mine.start()
    take, leave = post(row, sp, lambda rank: total, result_ref, sends.at[6], recvs.at[5])
    take()
    return leaves + [leave, mine.wait]


def step_kernel(frac_ref, labels_ref, cw_ref, cb_ref, ow_ref, ob_ref, grads_ref, loss_ref,
                z, pick, loss, out_sem, patch, labels, cw, cb, ow, ob, in_sems, send_sems, recv_sems,
                part, first, yslots, zslots, pieces, total,
                f0, f1, join, g, wide, owt, owb, act, d, low, grad, hot, early, dconv, dout, hsum, rsum):
    loads = [pltpu.make_async_copy(src, dst, in_sems.at[i]) for i, (src, dst) in enumerate(
        ((cw_ref, cw), (cb_ref, cb), (ow_ref, ow), (ob_ref, ob), (labels_ref, labels.at[pl.ds(0, PX)])))]
    team, row, ys, zs = rings()
    greet(loads, team, zs, ys[:SEC])
    arrive, leave = relay(team, frac_ref, patch, send_sems.at[7], recv_sems.at[6])
    for load in loads:
        load.wait()
    prepare(cw, cb, ow, ob, wide, owt, owb)
    clear(d, act, low, grad, dconv, dout, hsum, rsum, f0, f1, join)
    mark(labels, hot, SCALE)
    arrive()
    filter_patch(patch, f0, f1)
    stencil(f0, f1, join, g)
    train(hot, early, wide, owt, owb, g, act, d, low, grad, z, pick, dconv, dout, hsum, rsum, SCALE)
    finish(dconv, dout, hsum, rsum, part)

    def save_loss():
        losses(z, pick, loss, SCALE)
        pltpu.make_async_copy(loss, loss_ref, out_sem).start()

    leaves = reduce_grads(save_loss, row, ys, zs, part, first, yslots, zslots, pieces, total, grads_ref, send_sems, recv_sems)
    for end in [leave] + leaves:
        end()
    pltpu.make_async_copy(loss, loss_ref, out_sem).wait()


def train_step(frac, labels, cw, cb, ow, ob):
    far = pl.BlockSpec(memory_space=pl.ANY)
    dma = pltpu.SemaphoreType.DMA
    return pl.pallas_call(
        step_kernel,
        out_shape=(jax.ShapeDtypeStruct((SP, ROWS, 128), F32), jax.ShapeDtypeStruct((PX, PLANE), F32)),
        in_specs=[far] * 6,
        out_specs=(far, far),
        scratch_shapes=[
            pltpu.VMEM((PX + 8, PLANE), F32), pltpu.VMEM((PLANE // 128, 8 * PX, 128), F32), pltpu.VMEM((PX, PLANE), F32), dma,
            pltpu.VMEM((SP, 8 * SEC, 128), F32), pltpu.VMEM((PX + 8, PLANE), jnp.int32),
            pltpu.VMEM((FEATS, HID), BF16), pltpu.VMEM((HID,), F32), pltpu.VMEM((HID, BINS), BF16), pltpu.VMEM((BINS,), F32),
            dma((5,)), dma((8,)), dma((7,)),
            pltpu.VMEM((HID, 128), F32), pltpu.VMEM((SP, ROWS, 128), F32), pltpu.VMEM((2, Y, ROWS // 2, 128), F32),
            pltpu.VMEM((2, Z, ROWS // 2, 128), F32), pltpu.VMEM((4, ROWS // 2, 128), F32), pltpu.VMEM((ROWS, 128), F32),
        ] + compute_scratch(),
        compiler_params=pltpu.CompilerParams(collective_id=0, has_side_effects=True, vmem_limit_bytes=56 * 2**20),
        name="train_step",
    )(frac, labels, cw, cb, ow, ob)


def close_kernel(grads_ref, loss_in, loss_ref, conv_ref, cbias_ref, out_ref, obias_ref, grads, sems):
    loss = pltpu.make_async_copy(loss_in, loss_ref, sems.at[0])
    load = pltpu.make_async_copy(grads_ref, grads, sems.at[1])
    load.start()
    loss.start()
    load.wait()
    full = jnp.concatenate([grads[i] for i in range(SP)], axis=0)
    conv_ref[...] = full[:FEATS, :HID]
    cbias_ref[...] = full[FEATS:FEATS + 1, :HID].reshape(HID)
    obias_ref[...] = full[FEATS + 1:FEATS + 2, :HID].reshape(BINS)
    out_ref[...] = full[:, HID:]
    loss.wait()


def close(grads, loss):
    vm, far = pl.BlockSpec(memory_space=pltpu.VMEM), pl.BlockSpec(memory_space=pl.ANY)
    return pl.pallas_call(
        close_kernel,
        out_shape=(jax.ShapeDtypeStruct((PX, PLANE), F32), jax.ShapeDtypeStruct((FEATS, HID), F32),
                   jax.ShapeDtypeStruct((HID,), F32), jax.ShapeDtypeStruct((HID, BINS), F32),
                   jax.ShapeDtypeStruct((BINS,), F32)),
        in_specs=[far, far],
        out_specs=(vm, vm, vm, vm, vm),
        scratch_shapes=[pltpu.VMEM((SP, ROWS, 128), F32), pltpu.SemaphoreType.DMA((2,))],
        compiler_params=pltpu.CompilerParams(vmem_limit_bytes=56 * 2**20),
        name="close_step",
    )(grads, loss)


def shards(fraction, labels, conv_weight, conv_bias, out_weight, out_bias):
    blocks = fraction.reshape(TEAM, 4, 2, 128).transpose(0, 2, 1, 3).reshape(TEAM, 8, 128)
    grads, loss = train_step(blocks, labels.reshape(PX, PLANE),
                             conv_weight, conv_bias, out_weight, out_bias)
    loss, conv, cbias, out, obias = close(grads, loss)
    return loss.reshape(labels.shape), conv, cbias, out, obias


def solution(mesh):
    placed = (P("dp", None, "sp", "sec"), P("dp", ("sec", "sp"), None, None), P(), P(), P(), P())
    return jax.shard_map(
        shards,
        mesh=mesh,
        in_specs=placed,
        out_specs=(P("dp", ("sec", "sp"), None, None), P(), P(), P(), P()),
        check_vma=False,
    )
```
